32 devices in a mesh: row: 8 (over z, y), col: 4 (over x, core).
Axes of the slice: x: 2, y: 2, z: 4, core: 2. Of those that a mesh axis runs over, the one named last changes fastest.
Arguments:
- emb_source: bfloat16 [65536, 64], P('row'), may hold values from -0.625 to 0.625
- emb_target: bfloat16 [65536, 64], P(('col', 'row')), may hold values from -0.625 to 0.625
- source_mass: float32 [65536], P('row'), may hold values from 0.5 to 4
- target_mass: float32 [65536], P('col'), may hold values from 0.5 to 4
- start_potential: float32 [65536], P('col'), may hold values from -6 to 6
- support: int32 [512, 4, 4], P('row', 'col'), may hold values from 0 to 127, as said below
- count: int32 [512, 4], P('row', 'col'), may hold values from 1 to 4, as said below
Outputs:
- source_potential: float32 [65536], P('row')
- target_potential: float32 [65536], P('col')
The draws below stay inside these ranges and needn't reach their ends.
Inputs may be any that keep to these rules, and one draw needn't show every extreme that they name: support[r, c, k] names target block c * 128 + support[r, c, k]; the first count[r, c] entries of each list are distinct, and every target block is named by a live entry of some list. count[r, c] is the number of live entries of list (r, c).
All inputs are finite; a program needn't handle non-finite values.
Results may differ from the reference program's by a relative error of at most 0.0003.
Values may be sent and summed in bfloat16 or wider, within the bound.
No kernel may reach another device: no remote copies, remote signals or barrier semaphores. Data moves between devices by JAX's collectives and lax.ppermute only.
A program may use at most 64 MiB of HBM per device.

```python
import math
import jax
import jax.numpy as jnp
from jax import lax

D = 64
BLOCK = 128
KC = 4
TB_DEV = 128
RB = 512
NS = 65536
NT = 65536
N_COL = 4


def draw_support(key, part):
    first_key = jax.random.fold_in(key, 11)
    second_key = jax.random.fold_in(key, 23)
    orders = jax.vmap(lambda sub_key: jax.random.permutation(sub_key, TB_DEV))(jax.random.split(first_key, N_COL))
    row_ids = jnp.arange(RB, dtype=jnp.int32) % TB_DEV
    starts = jnp.transpose(orders[:, row_ids]).astype(jnp.int32)
    stride_top = (TB_DEV - 1) // (KC - 1) + 1
    strides = jax.random.randint(second_key, (RB, N_COL), 1, stride_top).astype(jnp.int32)
    steps_k = jnp.arange(KC, dtype=jnp.int32)[None, None, :]
    return ((starts[:, :, None] + strides[:, :, None] * steps_k) % TB_DEV).astype(jnp.int32)


def draw_count(key, part):
    sub_key = jax.random.fold_in(key, 37)
    counts = jax.random.randint(sub_key, (RB, N_COL), 1, KC + 1).astype(jnp.int32)
    return counts.at[0].set(KC)


def place_outliers(key, base, share):
    rows = base.shape[0]
    pick_key = jax.random.fold_in(key, 5)
    sign_key = jax.random.fold_in(key, 7)
    level_key = jax.random.fold_in(key, 9)
    outlying = jax.random.bernoulli(pick_key, share, (rows, 1))
    level = 0.625 * jnp.minimum(1.0, 0.4 + 0.8 * jax.random.uniform(level_key, (rows, 1), jnp.float32))
    signs = jnp.where(jax.random.bernoulli(sign_key, 0.5, base.shape), 1.0, -1.0)
    return jnp.where(outlying, signs * level, base).astype(jnp.bfloat16)


def draw_emb_source(key, part):
    own_key = jax.random.fold_in(key, 101)
    base_key = jax.random.fold_in(own_key, 3)
    base = jnp.clip(0.1 * jax.random.normal(base_key, (NS, D), jnp.float32), -0.3, 0.3)
    share = 0.0625
    return place_outliers(own_key, base, share)


def draw_emb_target(key, part):
    own_key = jax.random.fold_in(key, 201)
    base_key = jax.random.fold_in(own_key, 3)
    base = jnp.clip(0.1 * jax.random.normal(base_key, (NT, D), jnp.float32), -0.3, 0.3)
    share = 0.0625
    return place_outliers(own_key, base, share)


def draw_start_potential(key, part):
    own_key = jax.random.fold_in(key, 301)
    base_key = jax.random.fold_in(own_key, 3)
    first_key = jax.random.fold_in(own_key, 5)
    second_key = jax.random.fold_in(own_key, 7)
    gap_key = jax.random.fold_in(own_key, 9)
    base = jnp.clip(2.0 * jax.random.normal(base_key, (NT,), jnp.float32), -6.0, 6.0)
    blocks = NT // BLOCK
    first = jax.random.randint(first_key, (blocks, 1), 0, BLOCK).astype(jnp.int32)
    second = (first + jax.random.randint(second_key, (blocks, 1), 1, BLOCK).astype(jnp.int32)) % BLOCK
    gap = 0.05 * jax.random.uniform(gap_key, (blocks, 1), jnp.float32, 1.0, 3.0)
    position = jnp.arange(BLOCK, dtype=jnp.int32)[None, :]
    planted = jnp.where(position == first, 6.0, jnp.where(position == second, 6.0 - gap, base.reshape(blocks, BLOCK)))
    return planted.reshape(NT).astype(jnp.float32)


def level_of(key, dims, shards, least, top_value):
    loudness = 1.0
    for dim, blocks in shards:
        heights = jax.random.uniform(jax.random.fold_in(jax.random.fold_in(key, 6), dim), (blocks,), jnp.float32, least / len(shards), top_value / len(shards))
        loudness = loudness * jnp.repeat(jnp.exp(heights), dims[dim] // blocks).reshape((-1,) + (1,) * (len(dims) - 1 - dim))
    return loudness


def setup_inputs(seed: int = 0) -> dict:
    key_of = jax.random.split(jax.random.key(seed), 8)
    emb_source = draw_emb_source(jax.random.fold_in(key_of[7], 71), 0)
    emb_target = draw_emb_target(jax.random.fold_in(key_of[7], 71), 0)
    source_mass = jnp.clip(jnp.exp(math.log(4.0) - 2.0794415 * jax.random.uniform(key_of[2], (NS,), jnp.float32) ** level_of(key_of[2], (NS,), ((0, 8),), -0.2, 0.2)), 0.5, 4.0)
    target_mass = jnp.clip(jnp.exp(math.log(4.0) - 2.0794415 * jax.random.uniform(key_of[3], (NT,), jnp.float32) ** level_of(key_of[3], (NT,), ((0, 4),), -0.2, 0.2)), 0.5, 4.0)
    start_potential = draw_start_potential(jax.random.fold_in(key_of[7], 71), 0)
    support = draw_support(jax.random.fold_in(key_of[7], 71), 0)
    count = draw_count(jax.random.fold_in(key_of[7], 71), 0)
    return {"emb_source": emb_source, "emb_target": emb_target, "source_mass": source_mass, "target_mass": target_mass, "start_potential": start_potential, "support": support, "count": count}


entropy = 0.05
sentinel = -1.0e30


def tile_costs(source_block, target_tiles):
    source_f = source_block.astype(jnp.float32)
    target_f = target_tiles.astype(jnp.float32)
    cross_term = jnp.einsum("id,kjd->kij", source_f, target_f, precision=lax.Precision.HIGHEST)
    source_sq = jnp.sum(source_f * source_f, axis=-1)
    target_sq = jnp.sum(target_f * target_f, axis=-1)
    return 0.5 * (source_sq[None, :, None] + target_sq[:, None, :]) - cross_term


def layout(support, count):
    offsets = (jnp.arange(N_COL, dtype=jnp.int32) * TB_DEV)[None, :, None]
    global_ids = (support + offsets).reshape(RB, N_COL * KC)
    live_slots = (jnp.arange(KC, dtype=jnp.int32)[None, None, :] < count[:, :, None]).reshape(RB, N_COL * KC)
    return global_ids, live_slots


def source_update(emb_source, emb_target, target_pot, source_mass, global_ids, live_slots):
    source_blocks = emb_source.reshape(RB, BLOCK, D)
    target_blocks = emb_target.reshape(N_COL * TB_DEV, BLOCK, D)
    pot_blocks = target_pot.reshape(N_COL * TB_DEV, BLOCK)

    def one_block(items):
        source_block, block_ids, alive = items
        scores = (pot_blocks[block_ids][:, None, :] - tile_costs(source_block, target_blocks[block_ids])) / entropy
        scores = jnp.where(alive[:, None, None], scores, -jnp.inf)
        row_peak = jnp.max(scores, axis=(0, 2))
        row_total = jnp.sum(jnp.exp(scores - row_peak[None, :, None]), axis=(0, 2))
        return row_peak + jnp.log(row_total)

    lse_rows = lax.map(one_block, (source_blocks, global_ids, live_slots)).reshape(NS)
    return entropy * jnp.log(source_mass) - entropy * lse_rows


def target_update(emb_source, emb_target, source_pot, target_mass, global_ids, live_slots):
    source_blocks = emb_source.reshape(RB, BLOCK, D)
    target_blocks = emb_target.reshape(N_COL * TB_DEV, BLOCK, D)
    pot_rows = source_pot.reshape(RB, BLOCK)

    def one_block(items):
        source_block, pot_row, block_ids, alive = items
        scores = (pot_row[None, :, None] - tile_costs(source_block, target_blocks[block_ids])) / entropy
        col_peak = jnp.max(scores, axis=1)
        col_total = jnp.sum(jnp.exp(scores - col_peak[:, None, :]), axis=1)
        col_peak = jnp.where(alive[:, None], col_peak, sentinel)
        col_total = jnp.where(alive[:, None], col_total, 0.0)
        return col_peak, col_total

    col_peak, col_total = lax.map(one_block, (source_blocks, pot_rows, global_ids, live_slots))
    flat_ids = global_ids.reshape(-1)
    col_peak = col_peak.reshape(-1, BLOCK)
    col_total = col_total.reshape(-1, BLOCK)
    block_peak = jnp.full((N_COL * TB_DEV, BLOCK), sentinel, jnp.float32).at[flat_ids].max(col_peak)
    scaled = col_total * jnp.exp(col_peak - block_peak[flat_ids])
    block_total = jnp.zeros((N_COL * TB_DEV, BLOCK), jnp.float32).at[flat_ids].add(scaled)
    lse_cols = (block_peak + jnp.log(block_total)).reshape(NT)
    return entropy * jnp.log(target_mass) - entropy * lse_cols


def reference(emb_source, emb_target, source_mass, target_mass, start_potential, support, count):
    global_ids, live_slots = layout(support, count)
    first_f = source_update(emb_source, emb_target, start_potential, source_mass, global_ids, live_slots)
    first_g = target_update(emb_source, emb_target, first_f, target_mass, global_ids, live_slots)
    second_f = source_update(emb_source, emb_target, first_g, source_mass, global_ids, live_slots)
    second_g = target_update(emb_source, emb_target, second_f, target_mass, global_ids, live_slots)
    return second_f, second_g
```

```python
import functools

import jax
import jax.numpy as jnp
from jax import lax
from jax.experimental import pallas as pl
from jax.experimental.pallas import tpu as pltpu
from jax.sharding import PartitionSpec as P

BLOCK = 128
eps = 0.05
scale = 1.4426950408889634 / eps
unit = eps * 0.6931471805599453
floor = -1e30
group = 4


def merge(first, second):
    peak = jnp.maximum(first, second)
    gap = jnp.minimum(first, second) - peak
    return peak + unit * jnp.log2(1.0 + jnp.exp2(gap * scale))


def squares(block):
    wide = block.astype(jnp.float32)
    return jnp.sum(wide * wide, axis=0, keepdims=True)


def split_rows(pot):
    first = pot.astype(jnp.bfloat16).astype(jnp.float32)
    rest = pot - first
    second = rest.astype(jnp.bfloat16).astype(jnp.float32)
    third = rest - second
    rows = lax.broadcasted_iota(jnp.int32, (64, BLOCK), 0)
    out = jnp.where(rows == 0, first, jnp.where(rows == 1, second, jnp.where(rows == 2, third, 0.0)))
    return out.astype(jnp.bfloat16)


def one_rows():
    rows = lax.broadcasted_iota(jnp.int32, (64, BLOCK), 0)
    return jnp.where(rows < 3, 1.0, 0.0).astype(jnp.bfloat16)


def fill(count, step):
    def body(i, _):
        for k in range(4):
            step(i * 4 + k)
        return 0

    lax.fori_loop(0, count // 4, body, 0)


def tiles_lse(meta, slots, lhs, rhs, peaks, sums, top, tot, out):
    live = meta[0]

    def tile_step(i, _):
        for k in range(group):
            p = i * group + k
            z = jnp.dot(lhs[meta[2 + p]], rhs[meta[2 + slots + p]], preferred_element_type=jnp.float32)
            z = z.reshape(BLOCK // 8, 8, BLOCK)
            peak = jnp.max(z, axis=0)
            peaks[p] = peak
            sums[p] = jnp.sum(jnp.exp2((z - peak) * scale), axis=0)
        return 0

    lax.fori_loop(0, (live + group - 1) // group, tile_step, 0)
    top[...] = jnp.full(top.shape, floor, jnp.float32)
    tot[...] = jnp.full(tot.shape, 0.125, jnp.float32)

    def peak_step(p, carry):
        last, run = carry
        b = meta[2 + slots + p]
        run = jnp.where(b == last, jnp.maximum(run, peaks[p]), peaks[p])
        top[b] = run
        return b, run

    zero = jnp.zeros((8, BLOCK), jnp.float32)
    lax.fori_loop(0, live, peak_step, (jnp.int32(-1), zero))
    top[...] = jnp.broadcast_to(jnp.max(top[...], axis=1, keepdims=True), top.shape)

    def sum_step(p, carry):
        last, run = carry
        b = meta[2 + slots + p]
        part = sums[p] * jnp.exp2((peaks[p] - top[b]) * scale)
        run = jnp.where(b == last, run + part, part)
        tot[b] = run
        return b, run

    lax.fori_loop(0, live, sum_step, (jnp.int32(-1), zero))
    out[...] = top[:, 0, :] + unit * jnp.log2(jnp.sum(tot[...], axis=1))


def load_targets(meta, chunks, yt, sems):
    n = len(chunks)
    copies = []
    for k, chunk in enumerate(chunks):
        owner = lax.rem(meta[1] + n - k, n)
        copies.append(pltpu.make_async_copy(chunk, yt.at[owner], sems.at[k]))
    for copy in copies:
        copy.start()
    return copies


def target_block(yt, per, t):
    return yt[t // per, :, pl.ds(pl.multiple_of(lax.rem(t, per) * BLOCK, BLOCK), BLOCK)]


def source_kernel(n, first, slots, *refs):
    meta, xt, pot_in = refs[:3]
    refs = refs[3:]
    if not first:
        other, mass, ysq = refs[:3]
        refs = refs[3:]
    chunks, refs = refs[:n], refs[n:]
    if first:
        out, ysq, refs = refs[0], refs[1], refs[2:]
    else:
        out, refs = refs[0], refs[1:]
    yt, sems, lhs, rhs, peaks, sums, top, tot = refs
    copies = load_targets(meta, chunks, yt, sems)
    ones = one_rows()

    def fill_rhs(b):
        rhs[b, :64] = xt[:, pl.ds(pl.multiple_of(b * BLOCK, BLOCK), BLOCK)]
        rhs[b, 64:] = ones

    fill(rhs.shape[0], fill_rhs)
    for copy in copies:
        copy.wait()
    per = yt.shape[2] // BLOCK

    def fill_lhs(a):
        block = target_block(yt, per, a)
        if first:
            sq = squares(block)
            ysq[pl.ds(a, 1), :] = sq
            pot = pot_in[pl.ds(a, 1), :] - 0.5 * sq
        else:
            lse = merge(pot_in[pl.ds(a, 1), :], other[pl.ds(a, 1), :])
            pot = unit * jnp.log2(mass[pl.ds(a, 1), :]) - lse
        lhs[a] = jnp.concatenate([block, split_rows(pot)], axis=0).T

    fill(lhs.shape[0], fill_lhs)
    tiles_lse(meta, slots, lhs, rhs, peaks, sums, top, tot, out)


def target_kernel(n, slots, meta, xt, mine, other, mass, *refs):
    chunks, refs = refs[:n], refs[n:]
    out, pot_out, yt, sems, lhs, rhs, peaks, sums, top, tot = refs
    copies = load_targets(meta, chunks, yt, sems)
    ones = one_rows()

    def fill_lhs(a):
        block = xt[:, pl.ds(pl.multiple_of(a * BLOCK, BLOCK), BLOCK)]
        lse = merge(mine[pl.ds(a, 1), :], other[pl.ds(a, 1), :])
        pot = unit * jnp.log2(mass[pl.ds(a, 1), :]) - lse
        pot_out[pl.ds(a, 1), :] = pot + 0.5 * squares(block)
        lhs[a] = jnp.concatenate([block, split_rows(pot)], axis=0).T

    fill(lhs.shape[0], fill_lhs)
    for copy in copies:
        copy.wait()
    per = yt.shape[2] // BLOCK

    def fill_rhs(b):
        rhs[b, :64] = target_block(yt, per, b)
        rhs[b, 64:] = ones

    fill(rhs.shape[0], fill_rhs)
    tiles_lse(meta, slots, lhs, rhs, peaks, sums, top, tot, out)


def call(kernel, meta, dense, chunks, outs, blocks_a, blocks_b, slots, name):
    n = len(chunks)
    vmem = pl.BlockSpec(memory_space=pltpu.VMEM)
    return pl.pallas_call(
        kernel,
        out_shape=[jax.ShapeDtypeStruct(shape, jnp.float32) for shape in outs],
        in_specs=[pl.BlockSpec(memory_space=pltpu.SMEM)]
        + [vmem] * len(dense)
        + [pl.BlockSpec(memory_space=pl.ANY)] * n,
        out_specs=[vmem] * len(outs),
        scratch_shapes=[
            pltpu.VMEM((n,) + chunks[0].shape, jnp.bfloat16),
            pltpu.SemaphoreType.DMA((n,)),
            pltpu.VMEM((blocks_a, BLOCK, BLOCK), jnp.bfloat16),
            pltpu.VMEM((blocks_b, BLOCK, BLOCK), jnp.bfloat16),
            pltpu.VMEM((slots + group, 8, BLOCK), jnp.float32),
            pltpu.VMEM((slots + group, 8, BLOCK), jnp.float32),
            pltpu.VMEM((blocks_b, 8, BLOCK), jnp.float32),
            pltpu.VMEM((blocks_b, 8, BLOCK), jnp.float32),
        ],
        compiler_params=pltpu.CompilerParams(vmem_limit_bytes=48 * 1024 * 1024),
        name=name,
    )(meta, *dense, *chunks)


def exchange(value, axis, n):
    step = 1
    while True:
        other = lax.ppermute(value, axis, [(i, i ^ step) for i in range(n)])
        step *= 2
        if step >= n:
            return value, other
        value = merge(value, other)


def tile_list(code, alive, parts):
    slots = code.shape[0]
    code = jnp.where(alive, code, (1 << 30) + jnp.arange(slots, dtype=jnp.int32))
    rank = jnp.sum((code[None, :] < code[:, None]).astype(jnp.int32), axis=1)
    places = jnp.arange(slots, dtype=jnp.int32)
    hit = (rank[None, :] == places[:, None]) & alive[None, :]
    ordered = jnp.sum(jnp.where(hit, code[None, :], 0), axis=1)
    return ordered // parts, ordered % parts


def shards(rows, cols, emb_source, emb_target, source_mass, target_mass, start_potential, support, count):
    xt = emb_source.T
    mine = emb_target.T
    chunks = [mine]
    for k in range(1, rows):
        chunks.append(lax.ppermute(mine, "row", [(i, (i + k) % rows) for i in range(rows)]))
    sources = emb_source.shape[0] // BLOCK
    targets = start_potential.shape[0] // BLOCK
    depth = support.shape[2]
    slots = sources * depth
    t_ids = support.reshape(slots)
    r_ids = jnp.arange(slots, dtype=jnp.int32) // depth
    alive = (jnp.arange(depth, dtype=jnp.int32)[None, :] < count.reshape(sources, 1)).reshape(slots)
    live = jnp.sum(alive.astype(jnp.int32))
    me = lax.axis_index("row").astype(jnp.int32)
    head = jnp.stack([live, me])
    pad = jnp.zeros((group,), jnp.int32)
    s_b, s_a = tile_list(r_ids * targets + t_ids, alive, targets)
    t_b, t_a = tile_list(t_ids * sources + r_ids, alive, sources)
    width = slots + group
    s_meta = jnp.concatenate([head, s_a, pad, s_b, pad])
    t_meta = jnp.concatenate([head, t_a, pad, t_b, pad])
    s_mass = source_mass.reshape(sources, BLOCK)
    t_mass = target_mass.reshape(targets, BLOCK)
    s_shape, t_shape = (sources, BLOCK), (targets, BLOCK)

    lse, ysq = call(
        functools.partial(source_kernel, rows, True, width), s_meta,
        [xt, start_potential.reshape(t_shape)], chunks, [s_shape, t_shape],
        targets, sources, slots, "source_first",
    )
    pair = exchange(lse, "col", cols)
    lse, _ = call(
        functools.partial(target_kernel, rows, width), t_meta,
        [xt, *pair, s_mass], chunks, [t_shape, s_shape], sources, targets, slots, "target_first",
    )
    pair = exchange(lse, "row", rows)
    (lse,) = call(
        functools.partial(source_kernel, rows, False, width), s_meta,
        [xt, *pair, t_mass, ysq], chunks, [s_shape], targets, sources, slots, "source_second",
    )
    pair = exchange(lse, "col", cols)
    lse, second_f = call(
        functools.partial(target_kernel, rows, width), t_meta,
        [xt, *pair, s_mass], chunks, [t_shape, s_shape], sources, targets, slots, "target_second",
    )
    pair = exchange(lse, "row", rows)
    second_g = eps * jnp.log(t_mass) - merge(*pair) + 0.5 * ysq
    return second_f.reshape(-1), second_g.reshape(-1)


def solution(mesh):
    in_specs = (
        P("row", None),
        P(("col", "row"), None),
        P("row"),
        P("col"),
        P("col"),
        P("row", "col", None),
        P("row", "col"),
    )
    out_specs = (P("row"), P("col"))
    body = functools.partial(shards, mesh.shape["row"], mesh.shape["col"])
    return jax.shard_map(body, mesh=mesh, in_specs=in_specs, out_specs=out_specs, check_vma=False)
```

```python
import functools

import jax
import jax.numpy as jnp
from jax import lax
from jax.experimental import pallas as pl
from jax.experimental.pallas import tpu as pltpu
from jax.sharding import PartitionSpec as P

BLOCK = 128
eps = 0.05
scale = 1.4426950408889634 / eps
unit = eps * 0.6931471805599453
floor = -1e30
group = 16


def merge(first, second):
    peak = jnp.maximum(first, second)
    gap = jnp.minimum(first, second) - peak
    return peak + unit * jnp.log2(1.0 + jnp.exp2(gap * scale))


def squares(block):
    wide = block.astype(jnp.float32)
    return jnp.sum(wide * wide, axis=0, keepdims=True)


def split_rows(pot):
    first = pot.astype(jnp.bfloat16).astype(jnp.float32)
    rest = pot - first
    second = rest.astype(jnp.bfloat16).astype(jnp.float32)
    third = rest - second
    rows = lax.broadcasted_iota(jnp.int32, (64, BLOCK), 0)
    out = jnp.where(rows == 0, first, jnp.where(rows == 1, second, jnp.where(rows == 2, third, 0.0)))
    return out.astype(jnp.bfloat16)


def one_rows():
    rows = lax.broadcasted_iota(jnp.int32, (64, BLOCK), 0)
    return jnp.where(rows < 3, 1.0, 0.0).astype(jnp.bfloat16)


def fill(count, step):
    def body(i, _):
        for k in range(16):
            step(i * 16 + k)
        return 0

    lax.fori_loop(0, count // 16, body, 0)


def tiles_lse(meta, slots, lhs, rhs, peaks, sums, top, tot, out):
    live = meta[0]

    def tile_step(i, _):
        for k in range(group):
            p = i * group + k
            z = jnp.dot(lhs[meta[2 + p]], rhs[meta[2 + slots + p]], preferred_element_type=jnp.float32)
            z = z.reshape(BLOCK // 8, 8, BLOCK)
            peak = jnp.max(z, axis=0)
            peaks[p] = peak
            sums[p] = jnp.sum(jnp.exp2((z - peak) * scale), axis=0)
        return 0

    lax.fori_loop(0, (live + group - 1) // group, tile_step, 0)
    top[...] = jnp.full(top.shape, floor, jnp.float32)
    tot[...] = jnp.full(tot.shape, 0.125, jnp.float32)

    def peak_step(i, carry):
        last, run = carry
        for k in range(group):
            p = i * group + k
            b = meta[2 + slots + p]
            run = jnp.where(b == last, jnp.maximum(run, peaks[p]), peaks[p])
            top[b] = run
            last = b
        return last, run

    zero = jnp.zeros((8, BLOCK), jnp.float32)
    turns = (live + group - 1) // group
    lax.fori_loop(0, turns, peak_step, (jnp.int32(-1), zero))
    top[...] = jnp.broadcast_to(jnp.max(top[...], axis=1, keepdims=True), top.shape)

    def sum_step(i, carry):
        last, run = carry
        for k in range(group):
            p = i * group + k
            b = meta[2 + slots + p]
            part = sums[p] * jnp.exp2((peaks[p] - top[b]) * scale)
            run = jnp.where(b == last, run + part, part)
            tot[b] = run
            last = b
        return last, run

    lax.fori_loop(0, turns, sum_step, (jnp.int32(-1), zero))
    blocks = out.shape[0]
    lse = top[:, 0, :] + unit * jnp.log2(jnp.sum(tot[...], axis=1))
    out[...] = lse[:blocks]


def load_targets(meta, chunks, yt, sems):
    n = len(chunks)
    copies = []
    for k, chunk in enumerate(chunks):
        owner = lax.rem(meta[1] + n - k, n)
        copies.append(pltpu.make_async_copy(chunk, yt.at[owner], sems.at[k]))
    for copy in copies:
        copy.start()
    return copies


def target_block(yt, per, t):
    return yt[t // per, :, pl.ds(pl.multiple_of(lax.rem(t, per) * BLOCK, BLOCK), BLOCK)]


def source_kernel(n, first, slots, *refs):
    meta, xt, pot_in = refs[:3]
    refs = refs[3:]
    if not first:
        other, mass, ysq = refs[:3]
        refs = refs[3:]
    chunks, refs = refs[:n], refs[n:]
    if first:
        out, ysq, refs = refs[0], refs[1], refs[2:]
    else:
        out, refs = refs[0], refs[1:]
    yt, sems, lhs, rhs, peaks, sums, top, tot = refs
    copies = load_targets(meta, chunks, yt, sems)
    ones = one_rows()

    def fill_rhs(b):
        rhs[b, :64] = xt[:, pl.ds(pl.multiple_of(b * BLOCK, BLOCK), BLOCK)]
        rhs[b, 64:] = ones

    fill(rhs.shape[0] - 1, fill_rhs)
    for copy in copies:
        copy.wait()
    per = yt.shape[2] // BLOCK

    def fill_lhs(a):
        block = target_block(yt, per, a)
        if first:
            sq = squares(block)
            ysq[pl.ds(a, 1), :] = sq
            pot = pot_in[pl.ds(a, 1), :] - 0.5 * sq
        else:
            lse = merge(pot_in[pl.ds(a, 1), :], other[pl.ds(a, 1), :])
            pot = unit * jnp.log2(mass[pl.ds(a, 1), :]) - lse
        lhs[a] = jnp.concatenate([block, split_rows(pot)], axis=0).T

    fill(lhs.shape[0], fill_lhs)
    tiles_lse(meta, slots, lhs, rhs, peaks, sums, top, tot, out)


def target_kernel(n, slots, meta, xt, mine, other, mass, *refs):
    chunks, refs = refs[:n], refs[n:]
    out, pot_out, yt, sems, lhs, rhs, peaks, sums, top, tot = refs
    copies = load_targets(meta, chunks, yt, sems)
    ones = one_rows()

    def fill_lhs(a):
        block = xt[:, pl.ds(pl.multiple_of(a * BLOCK, BLOCK), BLOCK)]
        lse = merge(mine[pl.ds(a, 1), :], other[pl.ds(a, 1), :])
        pot = unit * jnp.log2(mass[pl.ds(a, 1), :]) - lse
        pot_out[pl.ds(a, 1), :] = pot + 0.5 * squares(block)
        lhs[a] = jnp.concatenate([block, split_rows(pot)], axis=0).T

    fill(lhs.shape[0], fill_lhs)
    for copy in copies:
        copy.wait()
    per = yt.shape[2] // BLOCK

    def fill_rhs(b):
        rhs[b, :64] = target_block(yt, per, b)
        rhs[b, 64:] = ones

    fill(rhs.shape[0] - 1, fill_rhs)
    tiles_lse(meta, slots, lhs, rhs, peaks, sums, top, tot, out)


def call(kernel, meta, dense, chunks, outs, blocks_a, blocks_b, slots, name):
    n = len(chunks)
    vmem = pl.BlockSpec(memory_space=pltpu.VMEM)
    return pl.pallas_call(
        kernel,
        out_shape=[jax.ShapeDtypeStruct(shape, jnp.float32) for shape in outs],
        in_specs=[pl.BlockSpec(memory_space=pltpu.SMEM)]
        + [vmem] * len(dense)
        + [pl.BlockSpec(memory_space=pl.ANY)] * n,
        out_specs=[vmem] * len(outs),
        scratch_shapes=[
            pltpu.VMEM((n,) + chunks[0].shape, jnp.bfloat16),
            pltpu.SemaphoreType.DMA((n,)),
            pltpu.VMEM((blocks_a, BLOCK, BLOCK), jnp.bfloat16),
            pltpu.VMEM((blocks_b + 1, BLOCK, BLOCK), jnp.bfloat16),
            pltpu.VMEM((slots + group, 8, BLOCK), jnp.float32),
            pltpu.VMEM((slots + group, 8, BLOCK), jnp.float32),
            pltpu.VMEM((blocks_b + 1, 8, BLOCK), jnp.float32),
            pltpu.VMEM((blocks_b + 1, 8, BLOCK), jnp.float32),
        ],
        compiler_params=pltpu.CompilerParams(vmem_limit_bytes=48 * 1024 * 1024),
        name=name,
    )(meta, *dense, *chunks)


def exchange(value, axis, n):
    step = 1
    while True:
        other = lax.ppermute(value, axis, [(i, i ^ step) for i in range(n)])
        step *= 2
        if step >= n:
            return value, other
        value = merge(value, other)


def tile_list(code, alive, parts, after):
    slots = code.shape[0]
    code = jnp.where(alive, code, (1 << 30) + jnp.arange(slots, dtype=jnp.int32))
    rank = jnp.sum((code[None, :] < code[:, None]).astype(jnp.int32), axis=1)
    places = jnp.arange(slots, dtype=jnp.int32)
    hit = (rank[None, :] == places[:, None]) & alive[None, :]
    ordered = jnp.sum(jnp.where(hit, code[None, :] - after, 0), axis=1) + after
    return ordered // parts, ordered % parts


def shards(rows, cols, emb_source, emb_target, source_mass, target_mass, start_potential, support, count):
    xt = emb_source.T
    mine = emb_target.T
    chunks = [mine]
    for k in range(1, rows):
        chunks.append(lax.ppermute(mine, "row", [(i, (i + k) % rows) for i in range(rows)]))
    sources = emb_source.shape[0] // BLOCK
    targets = start_potential.shape[0] // BLOCK
    depth = support.shape[2]
    slots = sources * depth
    t_ids = support.reshape(slots)
    r_ids = jnp.arange(slots, dtype=jnp.int32) // depth
    alive = (jnp.arange(depth, dtype=jnp.int32)[None, :] < count.reshape(sources, 1)).reshape(slots)
    live = jnp.sum(alive.astype(jnp.int32))
    me = lax.axis_index("row").astype(jnp.int32)
    head = jnp.stack([live, me])
    pad = jnp.zeros((group,), jnp.int32)
    s_b, s_a = tile_list(r_ids * targets + t_ids, alive, targets, sources * targets)
    t_b, t_a = tile_list(t_ids * sources + r_ids, alive, sources, sources * targets)
    width = slots + group
    s_meta = jnp.concatenate([head, s_a, pad, s_b, pad + sources])
    t_meta = jnp.concatenate([head, t_a, pad, t_b, pad + targets])
    s_mass = source_mass.reshape(sources, BLOCK)
    t_mass = target_mass.reshape(targets, BLOCK)
    s_shape, t_shape = (sources, BLOCK), (targets, BLOCK)

    lse, ysq = call(
        functools.partial(source_kernel, rows, True, width), s_meta,
        [xt, start_potential.reshape(t_shape)], chunks, [s_shape, t_shape],
        targets, sources, slots, "source_first",
    )
    pair = exchange(lse, "col", cols)
    lse, _ = call(
        functools.partial(target_kernel, rows, width), t_meta,
        [xt, *pair, s_mass], chunks, [t_shape, s_shape], sources, targets, slots, "target_first",
    )
    pair = exchange(lse, "row", rows)
    (lse,) = call(
        functools.partial(source_kernel, rows, False, width), s_meta,
        [xt, *pair, t_mass, ysq], chunks, [s_shape], targets, sources, slots, "source_second",
    )
    pair = exchange(lse, "col", cols)
    lse, second_f = call(
        functools.partial(target_kernel, rows, width), t_meta,
        [xt, *pair, s_mass], chunks, [t_shape, s_shape], sources, targets, slots, "target_second",
    )
    pair = exchange(lse, "row", rows)
    second_g = eps * jnp.log(t_mass) - merge(*pair) + 0.5 * ysq
    return second_f.reshape(-1), second_g.reshape(-1)


def solution(mesh):
    in_specs = (
        P("row", None),
        P(("col", "row"), None),
        P("row"),
        P("col"),
        P("col"),
        P("row", "col", None),
        P("row", "col"),
    )
    out_specs = (P("row"), P("col"))
    body = functools.partial(shards, mesh.shape["row"], mesh.shape["col"])
    return jax.shard_map(body, mesh=mesh, in_specs=in_specs, out_specs=out_specs, check_vma=False)
```

```python
import functools

import jax
import jax.numpy as jnp
from jax import lax
from jax.experimental import pallas as pl
from jax.experimental.pallas import tpu as pltpu
from jax.sharding import PartitionSpec as P

BLOCK = 128
eps = 0.05
scale = 1.4426950408889634 / eps
unit = eps * 0.6931471805599453
floor = -1e30
group = 8
turn = 2 * group
pad = 2 * turn


def merge(first, second):
    peak = jnp.maximum(first, second)
    gap = jnp.minimum(first, second) - peak
    return peak + unit * jnp.log2(1.0 + jnp.exp2(gap * scale))


def squares(block):
    wide = block.astype(jnp.float32)
    return jnp.sum(wide * wide, axis=0, keepdims=True)


def split_rows(pot):
    first = pot.astype(jnp.bfloat16).astype(jnp.float32)
    rest = pot - first
    second = rest.astype(jnp.bfloat16).astype(jnp.float32)
    third = rest - second
    rows = lax.broadcasted_iota(jnp.int32, (64, BLOCK), 0)
    out = jnp.where(rows == 0, first, jnp.where(rows == 1, second, jnp.where(rows == 2, third, 0.0)))
    return out.astype(jnp.bfloat16)


def one_rows():
    rows = lax.broadcasted_iota(jnp.int32, (64, BLOCK), 0)
    return jnp.where(rows < 3, 1.0, 0.0).astype(jnp.bfloat16)


def fill(count, step):
    def body(i, _):
        for k in range(16):
            step(i * 16 + k)
        return 0

    lax.fori_loop(0, count // 16, body, 0)


def tiles_lse(meta, slots, lhs, rhs, even, odd, peaks, sums, top, tot, out):
    turns = (meta[0] + turn - 1) // turn

    def dots(into, start):
        for k in range(group):
            a, b = meta[1 + start + k], meta[1 + slots + start + k]
            into[k] = jnp.dot(lhs[a], rhs[b], preferred_element_type=jnp.float32)

    def reduce(held, start):
        for k in range(group):
            z = held[k].reshape(BLOCK // 8, 8, BLOCK)
            peak = jnp.max(z, axis=0)
            peaks[start + k] = peak
            sums[start + k] = jnp.sum(jnp.exp2((z - peak) * scale), axis=0)

    def tile_step(i, _):
        start = i * turn
        dots(odd, start + group)
        reduce(even, start)
        dots(even, start + turn)
        reduce(odd, start + group)
        return 0

    dots(even, 0)
    lax.fori_loop(0, turns, tile_step, 0)
    top[...] = jnp.full(top.shape, floor, jnp.float32)
    tot[...] = jnp.full(tot.shape, 0.125, jnp.float32)

    def peak_step(i, carry):
        last, run = carry
        for k in range(turn):
            p = i * turn + k
            b = meta[1 + slots + p]
            run = jnp.where(b == last, jnp.maximum(run, peaks[p]), peaks[p])
            top[b] = run
            last = b
        return last, run

    zero = jnp.zeros((8, BLOCK), jnp.float32)
    lax.fori_loop(0, turns, peak_step, (jnp.int32(-1), zero))
    top[...] = jnp.broadcast_to(jnp.max(top[...], axis=1, keepdims=True), top.shape)

    def sum_step(i, carry):
        last, run = carry
        for k in range(turn):
            p = i * turn + k
            b = meta[1 + slots + p]
            part = sums[p] * jnp.exp2((peaks[p] - top[b]) * scale)
            run = jnp.where(b == last, run + part, part)
            tot[b] = run
            last = b
        return last, run

    lax.fori_loop(0, turns, sum_step, (jnp.int32(-1), zero))
    blocks = out.shape[0]
    lse = top[:, 0, :] + unit * jnp.log2(jnp.sum(tot[...], axis=1))
    out[...] = lse[:blocks]


def load_parts(parts, places, held, sems):
    copies = []
    for k, part in enumerate(parts):
        copies.append(pltpu.make_async_copy(part, held.at[places[k]], sems.at[k]))
        copies[-1].start()
    return copies


def block_of(held, i):
    per = held.shape[2] // BLOCK
    return held[i // per, :, pl.ds(pl.multiple_of(lax.rem(i, per) * BLOCK, BLOCK), BLOCK)]


def half_kernel(first, slots, n_src, n_tgt, source_side, *refs):
    (meta, places), refs = refs[:2], refs[2:]
    if first:
        (pot_in,), refs = refs[:1], refs[1:]
    else:
        (mine, other, mass), refs = refs[:3], refs[3:]
    srcs, refs = refs[:n_src], refs[n_src:]
    tgts, refs = refs[:n_tgt], refs[n_tgt:]
    (out, extra), refs = refs[:2], refs[2:]
    xs, ys, xsem, ysem, lhs, rhs, even, odd, peaks, sums, top, tot = refs
    half = xs.shape[2]
    pieces = [srcs[0].at[:, :half], srcs[0].at[:, half:]] + list(srcs[1:])
    x_copies = load_parts(pieces, [places[k] for k in range(n_src + 1)], xs, xsem)
    y_copies = load_parts(tgts, [places[n_src + 1 + k] for k in range(n_tgt)], ys, ysem)
    ones = one_rows()
    if source_side:
        a_held, a_copies, b_held, b_copies = ys, y_copies, xs, x_copies
    else:
        a_held, a_copies, b_held, b_copies = xs, x_copies, ys, y_copies

    def fill_rhs(b):
        rhs[b, :64] = block_of(b_held, b)
        rhs[b, 64:] = ones

    def fill_lhs(a):
        block = block_of(a_held, a)
        if first:
            sq = squares(block)
            extra[pl.ds(a, 1), :] = sq
            pot = pot_in[pl.ds(a, 1), :] - 0.5 * sq
        else:
            lse = merge(mine[pl.ds(a, 1), :], other[pl.ds(a, 1), :])
            pot = unit * jnp.log2(mass[pl.ds(a, 1), :]) - lse
            extra[pl.ds(a, 1), :] = pot
        lhs[a] = jnp.concatenate([block, split_rows(pot)], axis=0).T

    for copy in b_copies:
        copy.wait()
    fill(rhs.shape[0] - 1, fill_rhs)
    for copy in a_copies:
        copy.wait()
    fill(lhs.shape[0], fill_lhs)
    tiles_lse(meta, slots, lhs, rhs, even, odd, peaks, sums, top, tot, out)


def half_pass(source_side, meta, places, dense, srcs, tgts, sources, targets, slots, name):
    blocks_a, blocks_b = (targets, sources) if source_side else (sources, targets)
    vmem = pl.BlockSpec(memory_space=pltpu.VMEM)
    n_src, n_tgt = len(srcs), len(tgts)
    half = srcs[1].shape[1]
    shape = jax.ShapeDtypeStruct
    return pl.pallas_call(
        functools.partial(half_kernel, len(dense) == 1, slots + pad, n_src, n_tgt, source_side),
        out_shape=[shape((blocks_b, BLOCK), jnp.float32), shape((blocks_a, BLOCK), jnp.float32)],
        in_specs=[pl.BlockSpec(memory_space=pltpu.SMEM)] * 2
        + [vmem] * len(dense)
        + [pl.BlockSpec(memory_space=pl.ANY)] * (n_src + n_tgt),
        out_specs=[vmem, vmem],
        scratch_shapes=[
            pltpu.VMEM((n_src + 1, 64, half), jnp.bfloat16),
            pltpu.VMEM((n_tgt,) + tgts[0].shape, jnp.bfloat16),
            pltpu.SemaphoreType.DMA((n_src + 1,)),
            pltpu.SemaphoreType.DMA((n_tgt,)),
            pltpu.VMEM((blocks_a, BLOCK, BLOCK), jnp.bfloat16),
            pltpu.VMEM((blocks_b + 1, BLOCK, BLOCK), jnp.bfloat16),
            pltpu.VMEM((group, BLOCK, BLOCK), jnp.float32),
            pltpu.VMEM((group, BLOCK, BLOCK), jnp.float32),
            pltpu.VMEM((slots + turn, 8, BLOCK), jnp.float32),
            pltpu.VMEM((slots + turn, 8, BLOCK), jnp.float32),
            pltpu.VMEM((blocks_b + 1, 8, BLOCK), jnp.float32),
            pltpu.VMEM((blocks_b + 1, 8, BLOCK), jnp.float32),
        ],
        compiler_params=pltpu.CompilerParams(vmem_limit_bytes=48 * 1024 * 1024),
        name=name,
    )(meta, places, *dense, *srcs, *tgts)


def swap(value, axis, n, bit):
    return lax.ppermute(value, axis, [(i, i ^ bit) for i in range(n)])


def exchange(value, hops):
    for k, hop in enumerate(hops):
        other = swap(value, *hop)
        if k + 1 < len(hops):
            value = merge(value, other)
    return value, other


def tile_list(code, alive, parts, after):
    slots = code.shape[0]
    code = jnp.where(alive, code, (1 << 30) + jnp.arange(slots, dtype=jnp.int32))
    rank = jnp.sum((code[None, :] < code[:, None]).astype(jnp.int32), axis=1)
    places = jnp.arange(slots, dtype=jnp.int32)
    hit = (rank[None, :] == places[:, None]) & alive[None, :]
    ordered = jnp.sum(jnp.where(hit, code[None, :] - after, 0), axis=1) + after
    return ordered // parts, ordered % parts


def shards(rows, cols, emb_source, emb_target, source_mass, target_mass, start_potential, support, count):
    row = lax.axis_index("row").astype(jnp.int32)
    side, level = row % 2, row // 2
    core = lax.axis_index("col").astype(jnp.int32) % 2
    levels = rows // 2
    per = emb_target.shape[0] // BLOCK
    own_sources = emb_source.shape[0] // BLOCK
    sources, targets = 2 * own_sources, levels * per

    order = list(range(0, levels, 2)) + list(range(levels - 1 - levels % 2, 0, -2))
    after = {order[k]: order[(k + 1) % levels] for k in range(levels)}
    onward = [(2 * z + s, 2 * after[z] + s) for z in range(levels) for s in range(2)]
    back = [(b, a) for a, b in onward]
    place = jnp.asarray([order.index(z) for z in range(levels)], jnp.int32)[level]
    ring = jnp.asarray(order, jnp.int32)
    tgts, tgt_places = [emb_target.T], [level]
    ahead = behind = tgts[0]
    for step in range(1, levels // 2 + 1):
        ahead = lax.ppermute(ahead, "row", onward)
        tgts.append(ahead)
        tgt_places.append(ring[(place - step) % levels])
        if 2 * step < levels:
            behind = lax.ppermute(behind, "row", back)
            tgts.append(behind)
            tgt_places.append(ring[(place + step) % levels])

    xt = emb_source.T
    half = xt.shape[1] // 2
    part = lax.dynamic_slice(xt, (jnp.int32(0), core * half), (xt.shape[0], half))
    part = swap(part, "row", rows, 1)
    srcs = [xt, part, swap(part, "col", cols, 1)]
    far = 2 - 2 * side
    src_places = [2 * side, 2 * side + 1, far + core, far + 1 - core]
    places = jnp.stack(src_places + tgt_places)

    def both(mine):
        theirs = swap(mine, "row", rows, 1)
        return jnp.concatenate([jnp.where(side == 0, mine, theirs), jnp.where(side == 0, theirs, mine)])

    def of_side(whole):
        return lax.dynamic_index_in_dim(whole.reshape(levels, 2, per, BLOCK), side, 1, False).reshape(targets, BLOCK)

    depth = support.shape[2]
    slots = sources * depth
    named = support.reshape(own_sources, depth)
    named = jnp.where(jnp.arange(depth, dtype=jnp.int32)[None, :] < count, named, -1)
    named = both(named).reshape(slots)
    alive = (named >= 0) & ((named // per) % 2 == side)
    t_ids = (named // (2 * per)) * per + named % per
    s_ids = jnp.arange(slots, dtype=jnp.int32) // depth
    live = jnp.sum(alive.astype(jnp.int32)).reshape(1)
    blank = jnp.zeros((pad,), jnp.int32)
    s_b, s_a = tile_list(s_ids * targets + t_ids, alive, targets, sources * targets)
    t_b, t_a = tile_list(t_ids * sources + s_ids, alive, sources, sources * targets)
    s_meta = jnp.concatenate([live, s_a, blank, s_b, blank + sources])
    t_meta = jnp.concatenate([live, t_a, blank, t_b, blank + targets])
    s_mass = both(source_mass.reshape(own_sources, BLOCK))
    t_mass = of_side(target_mass)

    def sources_pass(dense, name):
        return half_pass(True, s_meta, places, dense, srcs, tgts, sources, targets, slots, name)

    def targets_pass(dense, name):
        return half_pass(False, t_meta, places, dense, srcs, tgts, sources, targets, slots, name)

    col_bits = [1 << k for k in range((cols - 1).bit_length())]
    row_bits = [1 << k for k in range((rows - 1).bit_length())]
    s_hops = [("col", cols, bit) for bit in col_bits] + [("row", rows, 1)]
    t_hops = [("row", rows, bit) for bit in row_bits[1:]]

    lse, ysq = sources_pass([of_side(start_potential)], "source_first")
    lse, _ = targets_pass([*exchange(lse, s_hops), s_mass], "target_first")
    lse, _ = sources_pass([*exchange(lse, t_hops), t_mass], "source_second")
    lse, pot = targets_pass([*exchange(lse, s_hops), s_mass], "target_second")
    second_g = eps * jnp.log(t_mass) - merge(*exchange(lse, t_hops)) + 0.5 * ysq
    other_g = swap(second_g, "row", rows, 1)
    first_g = jnp.where(side == 0, second_g, other_g).reshape(levels, 1, per, BLOCK)
    last_g = jnp.where(side == 0, other_g, second_g).reshape(levels, 1, per, BLOCK)
    second_g = jnp.concatenate([first_g, last_g], axis=1)
    xsq = squares(xt).reshape(own_sources, BLOCK)
    second_f = lax.dynamic_slice(pot, (side * own_sources, jnp.int32(0)), (own_sources, BLOCK)) + 0.5 * xsq
    return second_f.reshape(-1), second_g.reshape(-1)


def solution(mesh):
    in_specs = (
        P("row", None),
        P(("col", "row"), None),
        P("row"),
        P("col"),
        P("col"),
        P("row", "col", None),
        P("row", "col"),
    )
    out_specs = (P("row"), P("col"))
    body = functools.partial(shards, mesh.shape["row"], mesh.shape["col"])
    return jax.shard_map(body, mesh=mesh, in_specs=in_specs, out_specs=out_specs, check_vma=False)
```

```python
import functools

import jax
import jax.numpy as jnp
from jax import lax
from jax.experimental import pallas as pl
from jax.experimental.pallas import tpu as pltpu
from jax.sharding import PartitionSpec as P

BLOCK = 128
eps = 0.05
scale = 1.4426950408889634 / eps
unit = eps * 0.6931471805599453
floor = -1e30
turn = 16
longest = 64
pad = turn


def merge(first, second, third=None, fourth=None):
    peak = jnp.maximum(first, second)
    if third is not None:
        peak = jnp.maximum(peak, jnp.maximum(third, fourth))
    total = jnp.exp2((first - peak) * scale) + jnp.exp2((second - peak) * scale)
    if third is not None:
        total += jnp.exp2((third - peak) * scale) + jnp.exp2((fourth - peak) * scale)
    return peak + unit * jnp.log2(total)


def squares(block):
    wide = block.astype(jnp.float32)
    return jnp.sum(wide * wide, axis=0, keepdims=True)


def split_rows(pot):
    first = pot.astype(jnp.bfloat16).astype(jnp.float32)
    rest = pot - first
    second = rest.astype(jnp.bfloat16).astype(jnp.float32)
    third = rest - second
    rows = lax.broadcasted_iota(jnp.int32, (16, BLOCK), 0)
    out = jnp.where(rows == 0, first, jnp.where(rows == 1, second, jnp.where(rows == 2, third, 0.0)))
    return out.astype(jnp.bfloat16)


def one_rows():
    rows = lax.broadcasted_iota(jnp.int32, (16, BLOCK), 0)
    return jnp.where(rows < 3, 1.0, 0.0).astype(jnp.bfloat16)


def fill(count, step):
    def body(i, _):
        for k in range(16):
            step(i * 16 + k)
        return 0

    lax.fori_loop(0, count // 16, body, 0)


def tiles_lse(meta, a_at, b_at, lhs, tails, rhs, peaks, sums, top, tot, out):
    turns = (meta[0] + turn - 1) // turn
    ones = one_rows()
    last = rhs.shape[0] - 1

    def tiles(first, count):
        for k in range(count):
            p = first + k
            a, b = meta[a_at + p], meta[b_at + p]
            left = jnp.concatenate([lhs[a], tails[a]], axis=0)
            right = jnp.concatenate([rhs[jnp.minimum(b, last)], ones], axis=0)
            z = lax.dot_general(left, right, (((0,), (0,)), ((), ())), preferred_element_type=jnp.float32)
            z = z.reshape(BLOCK // 8, 8, BLOCK)
            peak = jnp.max(z, axis=0)
            peaks[p] = peak
            sums[p] = jnp.sum(jnp.exp2((z - peak) * scale), axis=0)

    def loop(first, count, size):
        def body(i, _):
            tiles(first + i * size, size)
            return 0

        lax.fori_loop(0, count, body, 0)
        return first + count * size

    many = turns // (longest // turn)
    left_over = turns - many * (longest // turn)
    done = loop(0, many, longest)
    done = loop(done, left_over // 2, 2 * turn)
    loop(done, lax.rem(left_over, 2), turn)
    top[...] = jnp.full(top.shape, floor, jnp.float32)
    tot[...] = jnp.full(tot.shape, 0.125, jnp.float32)

    def peak_step(i, carry):
        last, run = carry
        for k in range(turn):
            p = i * turn + k
            b = meta[b_at + p]
            run = jnp.where(b == last, jnp.maximum(run, peaks[p]), peaks[p])
            top[b] = run
            last = b
        return last, run

    zero = jnp.zeros((8, BLOCK), jnp.float32)
    lax.fori_loop(0, turns, peak_step, (jnp.int32(-1), zero))
    top[...] = jnp.broadcast_to(jnp.max(top[...], axis=1, keepdims=True), top.shape)

    def sum_step(i, carry):
        last, run = carry
        for k in range(turn):
            p = i * turn + k
            b = meta[b_at + p]
            part = sums[p] * jnp.exp2((peaks[p] - top[b]) * scale)
            run = jnp.where(b == last, run + part, part)
            tot[b] = run
            last = b
        return last, run

    lax.fori_loop(0, turns, sum_step, (jnp.int32(-1), zero))
    blocks = out.shape[0]
    lse = top[:, 0, :] + unit * jnp.log2(jnp.sum(tot[...], axis=1))
    out[...] = lse[:blocks]


def load_parts(parts, places, held, sems):
    copies = []
    for k, part in enumerate(parts):
        copies.append(pltpu.make_async_copy(part, held.at[places[k]], sems.at[k]))
        copies[-1].start()
    return copies


def block_of(held, i):
    per = held.shape[2] // BLOCK
    return held[i // per, :, pl.ds(pl.multiple_of(lax.rem(i, per) * BLOCK, BLOCK), BLOCK)]


def first_kernel(a_at, b_at, n_src, n_tgt, meta, places, pot_in, *refs):
    srcs, refs = refs[:n_src], refs[n_src:]
    tgts, refs = refs[:n_tgt], refs[n_tgt:]
    out, ysq, xb, yb, xs, ys, xsem, ysem, tails, peaks, sums, top, tot = refs
    half = xs.shape[2]
    pieces = [srcs[0].at[:, :half], srcs[0].at[:, half:]] + list(srcs[1:])
    x_copies = load_parts(pieces, [places[k] for k in range(n_src + 1)], xs, xsem)
    y_copies = load_parts(tgts, [places[n_src + 1 + k] for k in range(n_tgt)], ys, ysem)

    def fill_x(b):
        xb[b] = block_of(xs, b)

    def fill_y(a):
        block = block_of(ys, a)
        yb[a] = block
        sq = squares(block)
        ysq[pl.ds(a, 1), :] = sq
        tails[a] = split_rows(pot_in[pl.ds(a, 1), :] - 0.5 * sq)

    for copy in x_copies:
        copy.wait()
    fill(xb.shape[0], fill_x)
    for copy in y_copies:
        copy.wait()
    fill(yb.shape[0], fill_y)
    tiles_lse(meta, a_at, b_at, yb, tails, xb, peaks, sums, top, tot, out)


def later_kernel(a_at, b_at, n_parts, meta, *refs):
    parts, refs = refs[:n_parts], refs[n_parts:]
    mass, lhs, rhs, out, pot_out, tails, peaks, sums, top, tot = refs

    def fill_tails(a):
        lse = merge(*[part[pl.ds(a, 1), :] for part in parts])
        pot = unit * jnp.log2(mass[pl.ds(a, 1), :]) - lse
        pot_out[pl.ds(a, 1), :] = pot
        tails[a] = split_rows(pot)

    fill(lhs.shape[0], fill_tails)
    tiles_lse(meta, a_at, b_at, lhs, tails, rhs, peaks, sums, top, tot, out)


vmem = pl.BlockSpec(memory_space=pltpu.VMEM)
smem = pl.BlockSpec(memory_space=pltpu.SMEM)
far_off = pl.BlockSpec(memory_space=pltpu.HBM)


def tile_scratch(blocks_a, blocks_b, slots):
    return [
        pltpu.VMEM((blocks_a, 16, BLOCK), jnp.bfloat16),
        pltpu.VMEM((slots + pad, 8, BLOCK), jnp.float32),
        pltpu.VMEM((slots + pad, 8, BLOCK), jnp.float32),
        pltpu.VMEM((blocks_b + 1, 8, BLOCK), jnp.float32),
        pltpu.VMEM((blocks_b + 1, 8, BLOCK), jnp.float32),
    ]


def first_pass(meta, places, pot, srcs, tgts, sources, targets, slots, name):
    n_src, n_tgt = len(srcs), len(tgts)
    half = srcs[1].shape[1]
    shape = jax.ShapeDtypeStruct
    return pl.pallas_call(
        functools.partial(first_kernel, 1, 1 + slots + pad, n_src, n_tgt),
        out_shape=[
            shape((sources, BLOCK), jnp.float32),
            shape((targets, BLOCK), jnp.float32),
            shape((sources, 64, BLOCK), jnp.bfloat16),
            shape((targets, 64, BLOCK), jnp.bfloat16),
        ],
        in_specs=[smem, smem, vmem] + [far_off] * (n_src + n_tgt),
        out_specs=[vmem] * 4,
        scratch_shapes=[
            pltpu.VMEM((n_src + 1, 64, half), jnp.bfloat16),
            pltpu.VMEM((n_tgt,) + tgts[0].shape, jnp.bfloat16),
            pltpu.SemaphoreType.DMA((n_src + 1,)),
            pltpu.SemaphoreType.DMA((n_tgt,)),
        ]
        + tile_scratch(targets, sources, slots),
        compiler_params=pltpu.CompilerParams(vmem_limit_bytes=32 * 1024 * 1024),
        name=name,
    )(meta, places, pot, *srcs, *tgts)


def later_pass(meta, parts, mass, lhs, rhs, slots, order, name):
    blocks_a, blocks_b = lhs.shape[0], rhs.shape[0]
    shape = jax.ShapeDtypeStruct
    width = slots + pad
    a_at = 1 + 2 * order * width
    return pl.pallas_call(
        functools.partial(later_kernel, a_at, a_at + width, len(parts)),
        out_shape=[shape((blocks_b, BLOCK), jnp.float32), shape((blocks_a, BLOCK), jnp.float32)],
        in_specs=[smem] + [vmem] * (len(parts) + 3),
        out_specs=[vmem, vmem],
        scratch_shapes=tile_scratch(blocks_a, blocks_b, slots),
        compiler_params=pltpu.CompilerParams(vmem_limit_bytes=32 * 1024 * 1024),
        name=name,
    )(meta, *parts, mass, lhs, rhs)


def swap(value, rows, cols, row_bit, col_bit):
    if not col_bit:
        return lax.ppermute(value, "row", [(i, i ^ row_bit) for i in range(rows)])
    if not row_bit:
        return lax.ppermute(value, "col", [(i, i ^ col_bit) for i in range(cols)])
    pairs = [(i * cols + j, (i ^ row_bit) * cols + (j ^ col_bit)) for i in range(rows) for j in range(cols)]
    return lax.ppermute(value, ("row", "col"), pairs)


def exchange(value, hops, swap_by):
    for hop in hops[:-2]:
        value = merge(value, swap_by(value, *hop))
    if len(hops) == 1:
        return [value, swap_by(value, *hops[0])]
    first, second = hops[-2:]
    diagonal = (first[0] | second[0], first[1] | second[1])
    return [value, swap_by(value, *first), swap_by(value, *second), swap_by(value, *diagonal)]


def tile_list(code, alive, parts, after):
    slots = code.shape[0]
    code = jnp.where(alive, code, (1 << 30) + jnp.arange(slots, dtype=jnp.int32))
    rank = jnp.sum((code[None, :] < code[:, None]).astype(jnp.int32), axis=1)
    places = jnp.arange(slots, dtype=jnp.int32)
    hit = (rank[None, :] == places[:, None]) & alive[None, :]
    ordered = jnp.sum(jnp.where(hit, code[None, :] - after, 0), axis=1) + after
    return ordered // parts, ordered % parts


def shards(rows, cols, emb_source, emb_target, source_mass, target_mass, start_potential, support, count):
    row = lax.axis_index("row").astype(jnp.int32)
    side, level = row % 2, row // 2
    core = lax.axis_index("col").astype(jnp.int32) % 2
    levels = rows // 2
    per = emb_target.shape[0] // BLOCK
    own_sources = emb_source.shape[0] // BLOCK
    sources, targets = 2 * own_sources, levels * per

    order = list(range(0, levels, 2)) + list(range(levels - 1 - levels % 2, 0, -2))
    after = {order[k]: order[(k + 1) % levels] for k in range(levels)}
    onward = [(2 * z + s, 2 * after[z] + s) for z in range(levels) for s in range(2)]
    back = [(b, a) for a, b in onward]
    place = jnp.asarray([order.index(z) for z in range(levels)], jnp.int32)[level]
    ring = jnp.asarray(order, jnp.int32)
    tgts, tgt_places = [emb_target.T], [level]
    ahead = behind = tgts[0]
    for step in range(1, levels // 2 + 1):
        ahead = lax.ppermute(ahead, "row", onward)
        tgts.append(ahead)
        tgt_places.append(ring[(place - step) % levels])
        if 2 * step < levels:
            behind = lax.ppermute(behind, "row", back)
            tgts.append(behind)
            tgt_places.append(ring[(place + step) % levels])

    swap_by = lambda value, row_bit, col_bit: swap(value, rows, cols, row_bit, col_bit)
    depth = support.shape[2]
    slots = sources * depth
    named = support.reshape(own_sources, depth)
    named = jnp.where(jnp.arange(depth, dtype=jnp.int32)[None, :] < count, named, -1)
    mine = jnp.concatenate([source_mass.reshape(own_sources, BLOCK), named.astype(jnp.float32)], axis=1)

    xt, mine = lax.optimization_barrier((emb_source.T, mine))
    theirs = swap_by(mine, 1, 0)
    half = xt.shape[1] // 2
    part = lax.dynamic_slice(xt, (jnp.int32(0), core * half), (xt.shape[0], half))
    part = swap_by(part, 1, 0)
    srcs = [xt, part, swap_by(part, 0, 1)]
    far = 2 - 2 * side
    src_places = [2 * side, 2 * side + 1, far + core, far + 1 - core]
    places = jnp.stack(src_places + tgt_places)

    theirs, tgts[1] = lax.optimization_barrier((theirs, tgts[1]))
    pair = jnp.concatenate([jnp.where(side == 0, mine, theirs), jnp.where(side == 0, theirs, mine)])
    s_mass = pair[:, :BLOCK]
    named = pair[:, BLOCK:].astype(jnp.int32).reshape(slots)

    def of_side(whole):
        return lax.dynamic_index_in_dim(whole.reshape(levels, 2, per, BLOCK), side, 1, False).reshape(targets, BLOCK)

    alive = (named >= 0) & ((named // per) % 2 == side)
    t_ids = (named // (2 * per)) * per + named % per
    s_ids = jnp.arange(slots, dtype=jnp.int32) // depth
    live = jnp.sum(alive.astype(jnp.int32)).reshape(1)
    blank = jnp.zeros((pad,), jnp.int32)
    s_b, s_a = tile_list(s_ids * targets + t_ids, alive, targets, sources * targets)
    t_b, t_a = tile_list(t_ids * sources + s_ids, alive, sources, sources * targets)
    meta = jnp.concatenate([live, s_a, blank, s_b, blank + sources, t_a, blank, t_b, blank + targets])
    t_mass = of_side(target_mass)

    col_bits = [1 << k for k in range((cols - 1).bit_length())]
    row_bits = [1 << k for k in range((rows - 1).bit_length())]
    s_hops = [(0, bit) for bit in col_bits] + [(1, 0)]
    t_hops = [(bit, 0) for bit in row_bits[1:]]

    lse, ysq, xb, yb = first_pass(
        meta, places, of_side(start_potential), srcs, tgts, sources, targets, slots, "source_first"
    )
    lse, _ = later_pass(meta, exchange(lse, s_hops, swap_by), s_mass, xb, yb, slots, 1, "target_first")
    lse, _ = later_pass(meta, exchange(lse, t_hops, swap_by), t_mass, yb, xb, slots, 0, "source_second")
    lse, pot = later_pass(meta, exchange(lse, s_hops, swap_by), s_mass, xb, yb, slots, 1, "target_second")

    lse = lse - (eps * jnp.log(t_mass) + 0.5 * ysq)
    for hop in t_hops[:-1]:
        lse = merge(lse, swap_by(lse, *hop))
    last = t_hops[-1][0]
    own = merge(lse, swap_by(lse, last, 0)).reshape(levels, 1, per, BLOCK)
    other = merge(swap_by(lse, 1, 0), swap_by(lse, last | 1, 0)).reshape(levels, 1, per, BLOCK)
    second_g = -jnp.concatenate([jnp.where(side == 0, own, other), jnp.where(side == 0, other, own)], axis=1)
    xsq = squares(xt).reshape(own_sources, BLOCK)
    second_f = lax.dynamic_slice(pot, (side * own_sources, jnp.int32(0)), (own_sources, BLOCK)) + 0.5 * xsq
    return second_f.reshape(-1), second_g.reshape(-1)


def solution(mesh):
    in_specs = (
        P("row", None),
        P(("col", "row"), None),
        P("row"),
        P("col"),
        P("col"),
        P("row", "col", None),
        P("row", "col"),
    )
    out_specs = (P("row"), P("col"))
    body = functools.partial(shards, mesh.shape["row"], mesh.shape["col"])
    return jax.shard_map(body, mesh=mesh, in_specs=in_specs, out_specs=out_specs, check_vma=False)
```

```python
import functools

import jax
import jax.numpy as jnp
from jax import lax
from jax.experimental import pallas as pl
from jax.experimental.pallas import tpu as pltpu
from jax.sharding import PartitionSpec as P

BLOCK = 128
eps = 0.05
scale = 1.4426950408889634 / eps
unit = eps * 0.6931471805599453
floor = -1e30
turn = 16
longest = 64
pad = turn
place_bits = 12
place = 1 << place_bits


def merge(first, second, third=None, fourth=None):
    peak = jnp.maximum(first, second)
    if third is not None:
        peak = jnp.maximum(peak, jnp.maximum(third, fourth))
    total = jnp.exp2((first - peak) * scale) + jnp.exp2((second - peak) * scale)
    if third is not None:
        total += jnp.exp2((third - peak) * scale) + jnp.exp2((fourth - peak) * scale)
    return peak + unit * jnp.log2(total)


def squares(block):
    wide = block.astype(jnp.float32)
    return jnp.sum(wide * wide, axis=0, keepdims=True)


def rows_of(first, count, stride):
    return pl.ds(pl.multiple_of(first, 8), count) if stride == 1 else pl.ds(first, count, stride)


def store_split(tails, i, pot):
    first = pot.astype(jnp.bfloat16).astype(jnp.float32)
    rest = pot - first
    second = rest.astype(jnp.bfloat16).astype(jnp.float32)
    for k, part in enumerate((first, second, rest - second)):
        tails[pl.ds(i * 64 + k, 8, stride=8), :] = part


def one_rows():
    rows = lax.broadcasted_iota(jnp.int32, (16, BLOCK), 0)
    return jnp.where(rows < 3, 1.0, 0.0).astype(jnp.bfloat16)


def fill(count, step):
    def body(i, _):
        for k in range(16):
            step(i * 16 + k)
        return 0

    lax.fori_loop(0, count // 16, body, 0)


def fetch(tiles_in, listed, arrived):
    return pltpu.make_async_copy(tiles_in, listed, arrived)


def tiles_lse(tiles_in, listed, arrived, lhs, tails, rhs, top, tot, out):
    ones = one_rows()
    zeros = jnp.zeros((8, BLOCK), jnp.float32)
    end = rhs.shape[0] - 1
    top[...] = jnp.full(top.shape, floor, jnp.float32)
    tot[...] = jnp.full(tot.shape, 0.125, jnp.float32)
    fetch(tiles_in, listed, arrived).wait()
    turns = (listed[0] + turn - 1) // turn

    def tiles(first, count, carry):
        last, run, total = carry
        for k in range(count):
            code = listed[1 + first + k]
            a, b = code & (place - 1), code >> place_bits
            tail = jnp.concatenate([tails[rows_of(a * 8, 8, 1), :], zeros]).astype(jnp.bfloat16)
            left = jnp.concatenate([lhs[a], tail], axis=0)
            right = jnp.concatenate([rhs[jnp.minimum(b, end)], ones], axis=0)
            z = lax.dot_general(left, right, (((0,), (0,)), ((), ())), preferred_element_type=jnp.float32)
            z = z.reshape(BLOCK // 8, 8, BLOCK)
            peak = jnp.max(z, axis=0)
            part = jnp.sum(jnp.exp2((z - peak) * scale), axis=0)
            same = b == last
            joint = jnp.where(same, jnp.maximum(run, peak), peak)
            part = part * jnp.exp2((peak - joint) * scale)
            total = jnp.where(same, total * jnp.exp2((run - joint) * scale), 0.0) + part
            top[rows_of(b * 8, 8, 1), :] = joint
            tot[rows_of(b * 8, 8, 1), :] = total
            last, run = b, joint
        return last, run, total

    def loop(first, count, size, carry):
        return lax.fori_loop(0, count, lambda i, held: tiles(first + i * size, size, held), carry)

    many = turns // (longest // turn)
    left_over = turns - many * (longest // turn)
    carry = loop(0, many, longest, (jnp.int32(-1), zeros, zeros))
    done = many * longest
    carry = loop(done, left_over // 2, 2 * turn, carry)
    done += (left_over // 2) * 2 * turn
    loop(done, lax.rem(left_over, 2), turn, carry)

    for i in range(out.shape[0] // 8):
        peaks = [top[pl.ds(i * 64 + k, 8, stride=8), :] for k in range(8)]
        peak = functools.reduce(jnp.maximum, peaks)
        total = 0.0
        for k in range(8):
            total += tot[pl.ds(i * 64 + k, 8, stride=8), :] * jnp.exp2((peaks[k] - peak) * scale)
        out[i * 8 : i * 8 + 8, :] = peak + unit * jnp.log2(total)


def load_parts(parts, places, held, sems):
    copies = []
    for k, part in enumerate(parts):
        copies.append(pltpu.make_async_copy(part, held.at[places[k]], sems.at[k]))
        copies[-1].start()
    return copies


def block_of(held, i):
    per = held.shape[2] // BLOCK
    return held[i // per, :, pl.ds(pl.multiple_of(lax.rem(i, per) * BLOCK, BLOCK), BLOCK)]


def first_kernel(n_src, n_tgt, tiles_in, places, pot_in, *refs):
    srcs, refs = refs[:n_src], refs[n_src:]
    tgts, refs = refs[:n_tgt], refs[n_tgt:]
    out, ysq, xb, yb, xs, ys, xsem, ysem, listed, arrived, tails, top, tot = refs
    fetch(tiles_in, listed, arrived).start()
    half = xs.shape[2]
    pieces = [srcs[0].at[:, :half], srcs[0].at[:, half:]] + list(srcs[1:])
    x_copies = load_parts(pieces, [places[k] for k in range(n_src + 1)], xs, xsem)
    y_copies = load_parts(tgts, [places[n_src + 1 + k] for k in range(n_tgt)], ys, ysem)

    def fill_x(b):
        xb[b] = block_of(xs, b)

    def fill_y(a):
        block = block_of(ys, a)
        yb[a] = block
        sq = squares(block)
        ysq[pl.ds(a, 1), :] = sq

    for copy in x_copies:
        copy.wait()
    fill(xb.shape[0], fill_x)
    for copy in y_copies:
        copy.wait()
    fill(yb.shape[0], fill_y)
    tails[...] = jnp.zeros(tails.shape, jnp.float32)
    for i in range(yb.shape[0] // 8):
        rows = slice(i * 8, i * 8 + 8)
        store_split(tails, i, pot_in[rows, :] - 0.5 * ysq[rows, :])
    tiles_lse(tiles_in, listed, arrived, yb, tails, xb, top, tot, out)


def later_kernel(n_parts, keep, tiles_in, *refs):
    parts, refs = refs[:n_parts], refs[n_parts:]
    (mass, lhs, rhs, out), refs = refs[:4], refs[4:]
    if keep:
        (pot_out,), refs = refs[:1], refs[1:]
    listed, arrived, tails, top, tot = refs
    fetch(tiles_in, listed, arrived).start()
    tails[...] = jnp.zeros(tails.shape, jnp.float32)
    for i in range(lhs.shape[0] // 8):
        rows = slice(i * 8, i * 8 + 8)
        pot = unit * jnp.log2(mass[rows, :]) - merge(*[part[rows, :] for part in parts])
        if keep:
            pot_out[rows, :] = pot
        store_split(tails, i, pot)
    tiles_lse(tiles_in, listed, arrived, lhs, tails, rhs, top, tot, out)


vmem = pl.BlockSpec(memory_space=pltpu.VMEM)
smem = pl.BlockSpec(memory_space=pltpu.SMEM)
far_off = pl.BlockSpec(memory_space=pltpu.HBM)


def tile_scratch(blocks_a, blocks_b, listed):
    return [
        pltpu.SMEM((listed,), jnp.int32),
        pltpu.SemaphoreType.DMA,
        pltpu.VMEM((blocks_a * 8, BLOCK), jnp.float32),
        pltpu.VMEM((blocks_b * 8 + 8, BLOCK), jnp.float32),
        pltpu.VMEM((blocks_b * 8 + 8, BLOCK), jnp.float32),
    ]


def first_pass(listed, places, pot, srcs, tgts, sources, targets, name):
    n_src, n_tgt = len(srcs), len(tgts)
    half = srcs[1].shape[1]
    shape = jax.ShapeDtypeStruct
    return pl.pallas_call(
        functools.partial(first_kernel, n_src, n_tgt),
        out_shape=[
            shape((sources, BLOCK), jnp.float32),
            shape((targets, BLOCK), jnp.float32),
            shape((sources, 64, BLOCK), jnp.bfloat16),
            shape((targets, 64, BLOCK), jnp.bfloat16),
        ],
        in_specs=[far_off, smem, vmem] + [far_off] * (n_src + n_tgt),
        out_specs=[vmem] * 4,
        scratch_shapes=[
            pltpu.VMEM((n_src + 1, 64, half), jnp.bfloat16),
            pltpu.VMEM((n_tgt,) + tgts[0].shape, jnp.bfloat16),
            pltpu.SemaphoreType.DMA((n_src + 1,)),
            pltpu.SemaphoreType.DMA((n_tgt,)),
        ]
        + tile_scratch(targets, sources, listed.shape[0]),
        compiler_params=pltpu.CompilerParams(vmem_limit_bytes=32 * 1024 * 1024),
        name=name,
    )(listed, places, pot, *srcs, *tgts)


def later_pass(listed, parts, mass, lhs, rhs, keep, name):
    blocks_a, blocks_b = lhs.shape[0], rhs.shape[0]
    shapes = [(blocks_b, BLOCK)] + [(blocks_a, BLOCK)] * keep
    return pl.pallas_call(
        functools.partial(later_kernel, len(parts), keep),
        out_shape=[jax.ShapeDtypeStruct(shape, jnp.float32) for shape in shapes],
        in_specs=[far_off] + [vmem] * (len(parts) + 3),
        out_specs=[vmem] * len(shapes),
        scratch_shapes=tile_scratch(blocks_a, blocks_b, listed.shape[0]),
        compiler_params=pltpu.CompilerParams(vmem_limit_bytes=32 * 1024 * 1024),
        name=name,
    )(listed, *parts, mass, lhs, rhs)


def swap(value, rows, cols, row_bit, col_bit):
    if not col_bit:
        return lax.ppermute(value, "row", [(i, i ^ row_bit) for i in range(rows)])
    if not row_bit:
        return lax.ppermute(value, "col", [(i, i ^ col_bit) for i in range(cols)])
    pairs = [(i * cols + j, (i ^ row_bit) * cols + (j ^ col_bit)) for i in range(rows) for j in range(cols)]
    return lax.ppermute(value, ("row", "col"), pairs)


def exchange(value, hops, swap_by):
    for hop in hops[:-2]:
        value = merge(value, swap_by(value, *hop))
    if len(hops) == 1:
        return [value, swap_by(value, *hops[0])]
    first, second = hops[-2:]
    diagonal = (first[0] | second[0], first[1] | second[1])
    return [value, swap_by(value, *first), swap_by(value, *second), swap_by(value, *diagonal)]


def tile_list(code, alive, parts, after):
    slots = code.shape[0]
    code = jnp.where(alive, code, (1 << 30) + jnp.arange(slots, dtype=jnp.int32))
    rank = jnp.sum((code[None, :] < code[:, None]).astype(jnp.int32), axis=1)
    places = jnp.arange(slots, dtype=jnp.int32)
    hit = (rank[None, :] == places[:, None]) & alive[None, :]
    ordered = jnp.sum(jnp.where(hit, code[None, :] - after, 0), axis=1) + after
    return place * (ordered // parts) + ordered % parts


def shards(rows, cols, emb_source, emb_target, source_mass, target_mass, start_potential, support, count):
    row = lax.axis_index("row").astype(jnp.int32)
    side, level = row % 2, row // 2
    core = lax.axis_index("col").astype(jnp.int32) % 2
    levels = rows // 2
    per = emb_target.shape[0] // BLOCK
    own_sources = emb_source.shape[0] // BLOCK
    sources, targets = 2 * own_sources, levels * per

    order = list(range(0, levels, 2)) + list(range(levels - 1 - levels % 2, 0, -2))
    after = {order[k]: order[(k + 1) % levels] for k in range(levels)}
    onward = [(2 * z + s, 2 * after[z] + s) for z in range(levels) for s in range(2)]
    back = [(b, a) for a, b in onward]
    place = jnp.asarray([order.index(z) for z in range(levels)], jnp.int32)[level]
    ring = jnp.asarray(order, jnp.int32)
    tgts, tgt_places = [emb_target.T], [level]
    ahead = behind = tgts[0]
    for step in range(1, levels // 2 + 1):
        ahead = lax.ppermute(ahead, "row", onward)
        tgts.append(ahead)
        tgt_places.append(ring[(place - step) % levels])
        if 2 * step < levels:
            behind = lax.ppermute(behind, "row", back)
            tgts.append(behind)
            tgt_places.append(ring[(place + step) % levels])

    swap_by = lambda value, row_bit, col_bit: swap(value, rows, cols, row_bit, col_bit)
    depth = support.shape[2]
    slots = sources * depth
    named = support.reshape(own_sources, depth)
    named = jnp.where(jnp.arange(depth, dtype=jnp.int32)[None, :] < count, named, -1)
    mine = jnp.concatenate([source_mass.reshape(own_sources, BLOCK), named.astype(jnp.float32)], axis=1)

    xt, mine = lax.optimization_barrier((emb_source.T, mine))
    theirs = swap_by(mine, 1, 0)
    half = xt.shape[1] // 2
    part = lax.dynamic_slice(xt, (jnp.int32(0), core * half), (xt.shape[0], half))
    part = swap_by(part, 1, 0)
    srcs = [xt, part, swap_by(part, 0, 1)]
    far = 2 - 2 * side
    src_places = [2 * side, 2 * side + 1, far + core, far + 1 - core]
    places = jnp.stack(src_places + tgt_places)

    theirs, tgts[1] = lax.optimization_barrier((theirs, tgts[1]))
    pair = jnp.concatenate([jnp.where(side == 0, mine, theirs), jnp.where(side == 0, theirs, mine)])
    s_mass = pair[:, :BLOCK]
    named = pair[:, BLOCK:].astype(jnp.int32).reshape(slots)

    def of_side(whole):
        return lax.dynamic_index_in_dim(whole.reshape(levels, 2, per, BLOCK), side, 1, False).reshape(targets, BLOCK)

    alive = (named >= 0) & ((named // per) % 2 == side)
    t_ids = (named // (2 * per)) * per + named % per
    s_ids = jnp.arange(slots, dtype=jnp.int32) // depth
    live = jnp.sum(alive.astype(jnp.int32)).reshape(1)
    last = jnp.full((pad,), place, jnp.int32)
    by_source = tile_list(s_ids * targets + t_ids, alive, targets, sources * targets)
    by_source = jnp.concatenate([live, by_source, last * sources])
    by_target = tile_list(t_ids * sources + s_ids, alive, sources, sources * targets)
    by_target = jnp.concatenate([live, by_target, last * targets])
    by_source, by_target = lax.optimization_barrier((by_source, by_target))
    t_mass = of_side(target_mass)

    col_bits = [1 << k for k in range((cols - 1).bit_length())]
    row_bits = [1 << k for k in range((rows - 1).bit_length())]
    s_hops = [(0, bit) for bit in col_bits] + [(1, 0)]
    t_hops = [(bit, 0) for bit in row_bits[1:]]

    lse, ysq, xb, yb = first_pass(
        by_source, places, of_side(start_potential), srcs, tgts, sources, targets, "source_first"
    )
    (lse,) = later_pass(by_target, exchange(lse, s_hops, swap_by), s_mass, xb, yb, False, "target_first")
    (lse,) = later_pass(by_source, exchange(lse, t_hops, swap_by), t_mass, yb, xb, False, "source_second")
    lse, pot = later_pass(by_target, exchange(lse, s_hops, swap_by), s_mass, xb, yb, True, "target_second")

    lse = lse - (eps * jnp.log(t_mass) + 0.5 * ysq)
    for hop in t_hops[:-1]:
        lse = merge(lse, swap_by(lse, *hop))
    last = t_hops[-1][0]
    own = merge(lse, swap_by(lse, last, 0)).reshape(levels, 1, per, BLOCK)
    other = merge(swap_by(lse, 1, 0), swap_by(lse, last | 1, 0)).reshape(levels, 1, per, BLOCK)
    second_g = -jnp.concatenate([jnp.where(side == 0, own, other), jnp.where(side == 0, other, own)], axis=1)
    xsq = squares(xt).reshape(own_sources, BLOCK)
    second_f = lax.dynamic_slice(pot, (side * own_sources, jnp.int32(0)), (own_sources, BLOCK)) + 0.5 * xsq
    return second_f.reshape(-1), second_g.reshape(-1)


def solution(mesh):
    in_specs = (
        P("row", None),
        P(("col", "row"), None),
        P("row"),
        P("col"),
        P("col"),
        P("row", "col", None),
        P("row", "col"),
    )
    out_specs = (P("row"), P("col"))
    body = functools.partial(shards, mesh.shape["row"], mesh.shape["col"])
    return jax.shard_map(body, mesh=mesh, in_specs=in_specs, out_specs=out_specs, check_vma=False)
```

```python
import functools

import jax
import jax.numpy as jnp
from jax import lax
from jax.experimental import pallas as pl
from jax.experimental.pallas import tpu as pltpu
from jax.sharding import PartitionSpec as P

BLOCK = 128
eps = 0.05
scale = 1.4426950408889634 / eps
unit = eps * 0.6931471805599453
floor = -1e30
turn = 16
longest = 64
pad = turn
place_bits = 12
place = 1 << place_bits


def merge(first, second, third=None, fourth=None):
    peak = jnp.maximum(first, second)
    if third is not None:
        peak = jnp.maximum(peak, jnp.maximum(third, fourth))
    total = jnp.exp2((first - peak) * scale) + jnp.exp2((second - peak) * scale)
    if third is not None:
        total += jnp.exp2((third - peak) * scale) + jnp.exp2((fourth - peak) * scale)
    return peak + unit * jnp.log2(total)


def squares(block):
    wide = block.astype(jnp.float32)
    return jnp.sum(wide * wide, axis=0, keepdims=True)


def rows_of(first, count, stride):
    return pl.ds(pl.multiple_of(first, 8), count) if stride == 1 else pl.ds(first, count, stride)


def store_split(tails, i, pot):
    first = pot.astype(jnp.bfloat16).astype(jnp.float32)
    rest = pot - first
    second = rest.astype(jnp.bfloat16).astype(jnp.float32)
    for k, part in enumerate((first, second, rest - second)):
        tails[pl.ds(i * 64 + k, 8, stride=8), :] = part


def one_rows():
    rows = lax.broadcasted_iota(jnp.int32, (16, BLOCK), 0)
    return jnp.where(rows < 3, 1.0, 0.0).astype(jnp.bfloat16)


def fetch(tiles_in, listed, arrived):
    return pltpu.make_async_copy(tiles_in, listed, arrived)


def tiles_lse(tiles_in, listed, arrived, lhs, tails, rhs, top, tot, out):
    ones = one_rows()
    zeros = jnp.zeros((8, BLOCK), jnp.float32)
    end = rhs.shape[0] - 1
    top[...] = jnp.full(top.shape, floor, jnp.float32)
    tot[...] = jnp.full(tot.shape, 0.125, jnp.float32)
    fetch(tiles_in, listed, arrived).wait()
    turns = (listed[0] + turn - 1) // turn

    def tiles(first, count, carry):
        last, run, total = carry
        for k in range(count):
            code = listed[1 + first + k]
            a, b = code & (place - 1), code >> place_bits
            tail = jnp.concatenate([tails[rows_of(a * 8, 8, 1), :], zeros]).astype(jnp.bfloat16)
            left = jnp.concatenate([lhs[a], tail], axis=0)
            right = jnp.concatenate([rhs[jnp.minimum(b, end)], ones], axis=0)
            z = lax.dot_general(left, right, (((0,), (0,)), ((), ())), preferred_element_type=jnp.float32)
            z = z.reshape(BLOCK // 8, 8, BLOCK)
            peak = jnp.max(z, axis=0)
            same = b == last
            joint = jnp.where(same, jnp.maximum(run, peak), peak)
            part = jnp.sum(jnp.exp2((z - joint) * scale), axis=0)
            total = jnp.where(same, total * jnp.exp2((run - joint) * scale), 0.0) + part
            top[rows_of(b * 8, 8, 1), :] = joint
            tot[rows_of(b * 8, 8, 1), :] = total
            last, run = b, joint
        return last, run, total

    def loop(first, count, size, carry):
        return lax.fori_loop(0, count, lambda i, held: tiles(first + i * size, size, held), carry)

    many = turns // (longest // turn)
    left_over = turns - many * (longest // turn)
    carry = loop(0, many, longest, (jnp.int32(-1), zeros, zeros))
    done = many * longest
    carry = loop(done, left_over // 2, 2 * turn, carry)
    done += (left_over // 2) * 2 * turn
    loop(done, lax.rem(left_over, 2), turn, carry)

    for i in range(out.shape[0] // 8):
        peaks = [top[pl.ds(i * 64 + k, 8, stride=8), :] for k in range(8)]
        peak = functools.reduce(jnp.maximum, peaks)
        total = 0.0
        for k in range(8):
            total += tot[pl.ds(i * 64 + k, 8, stride=8), :] * jnp.exp2((peaks[k] - peak) * scale)
        out[i * 8 : i * 8 + 8, :] = peak + unit * jnp.log2(total)


def ring_place(level, levels):
    return jnp.where(level % 2 == 0, level // 2, levels - (level + 1) // 2)


def ring_level(place, levels):
    place = lax.rem(place + levels, levels)
    return jnp.where(place < (levels + 1) // 2, 2 * place, 2 * (levels - place) - 1)


def first_kernel(n_src, n_tgt, levels, steps, here, tiles_in, pot_in, *refs):
    srcs, refs = refs[:n_src], refs[n_src:]
    tgts, refs = refs[:n_tgt], refs[n_tgt:]
    out, ysq, xb, yb, listed, arrived, tails, top, tot = refs
    fetch(tiles_in, listed, arrived).start()
    side, level, core = here[0], here[1], here[2]
    half = srcs[1].shape[1]
    far = 2 - 2 * side
    pieces = ((srcs[0], 0, 2 * side), (srcs[0], half, 2 * side + 1), (srcs[1], 0, far + core), (srcs[2], 0, far + 1 - core))
    for part, first, where in pieces:
        for j in range(half // BLOCK):
            xb[where * (half // BLOCK) + j] = part[:, first + j * BLOCK : first + (j + 1) * BLOCK]
    per = tgts[0].shape[1] // BLOCK
    for part, step in zip(tgts, steps):
        where = ring_level(ring_place(level, levels) + step, levels)
        for j in range(per):
            block = part[:, j * BLOCK : (j + 1) * BLOCK]
            yb[where * per + j] = block
            ysq[pl.ds(where * per + j, 1), :] = squares(block)
    tails[...] = jnp.zeros(tails.shape, jnp.float32)
    for i in range(yb.shape[0] // 8):
        rows = slice(i * 8, i * 8 + 8)
        store_split(tails, i, pot_in[rows, :] - 0.5 * ysq[rows, :])
    tiles_lse(tiles_in, listed, arrived, yb, tails, xb, top, tot, out)


def later_kernel(n_parts, keep, tiles_in, *refs):
    parts, refs = refs[:n_parts], refs[n_parts:]
    (mass, lhs, rhs, out), refs = refs[:4], refs[4:]
    if keep:
        (pot_out,), refs = refs[:1], refs[1:]
    listed, arrived, tails, top, tot = refs
    fetch(tiles_in, listed, arrived).start()
    tails[...] = jnp.zeros(tails.shape, jnp.float32)
    for i in range(lhs.shape[0] // 8):
        rows = slice(i * 8, i * 8 + 8)
        pot = unit * jnp.log2(mass[rows, :]) - merge(*[part[rows, :] for part in parts])
        if keep:
            pot_out[rows, :] = pot
        store_split(tails, i, pot)
    tiles_lse(tiles_in, listed, arrived, lhs, tails, rhs, top, tot, out)


vmem = pl.BlockSpec(memory_space=pltpu.VMEM)
smem = pl.BlockSpec(memory_space=pltpu.SMEM)


def tile_scratch(blocks_a, blocks_b, listed):
    return [
        pltpu.SMEM((listed,), jnp.int32),
        pltpu.SemaphoreType.DMA,
        pltpu.VMEM((blocks_a * 8, BLOCK), jnp.float32),
        pltpu.VMEM((blocks_b * 8 + 8, BLOCK), jnp.float32),
        pltpu.VMEM((blocks_b * 8 + 8, BLOCK), jnp.float32),
    ]


def first_pass(listed, here, pot, srcs, tgts, steps, sources, targets, name):
    n_src, n_tgt = len(srcs), len(tgts)
    shape = jax.ShapeDtypeStruct
    return pl.pallas_call(
        functools.partial(first_kernel, n_src, n_tgt, targets * BLOCK // tgts[0].shape[1], steps),
        out_shape=[
            shape((sources, BLOCK), jnp.float32),
            shape((targets, BLOCK), jnp.float32),
            shape((sources, 64, BLOCK), jnp.bfloat16),
            shape((targets, 64, BLOCK), jnp.bfloat16),
        ],
        in_specs=[smem, vmem, vmem] + [vmem] * (n_src + n_tgt),
        out_specs=[vmem] * 4,
        scratch_shapes=tile_scratch(targets, sources, listed.shape[0]),
        compiler_params=pltpu.CompilerParams(vmem_limit_bytes=32 * 1024 * 1024),
        name=name,
    )(here, listed, pot, *srcs, *tgts)


def later_pass(listed, parts, mass, lhs, rhs, keep, name):
    blocks_a, blocks_b = lhs.shape[0], rhs.shape[0]
    shapes = [(blocks_b, BLOCK)] + [(blocks_a, BLOCK)] * keep
    return pl.pallas_call(
        functools.partial(later_kernel, len(parts), keep),
        out_shape=[jax.ShapeDtypeStruct(shape, jnp.float32) for shape in shapes],
        in_specs=[vmem] + [vmem] * (len(parts) + 3),
        out_specs=[vmem] * len(shapes),
        scratch_shapes=tile_scratch(blocks_a, blocks_b, listed.shape[0]),
        compiler_params=pltpu.CompilerParams(vmem_limit_bytes=32 * 1024 * 1024),
        name=name,
    )(listed, *parts, mass, lhs, rhs)


def swap(value, rows, cols, row_bit, col_bit):
    if not col_bit:
        return lax.ppermute(value, "row", [(i, i ^ row_bit) for i in range(rows)])
    if not row_bit:
        return lax.ppermute(value, "col", [(i, i ^ col_bit) for i in range(cols)])
    pairs = [(i * cols + j, (i ^ row_bit) * cols + (j ^ col_bit)) for i in range(rows) for j in range(cols)]
    return lax.ppermute(value, ("row", "col"), pairs)


def exchange(value, hops, swap_by):
    for hop in hops[:-2]:
        value = merge(value, swap_by(value, *hop))
    if len(hops) == 1:
        return [value, swap_by(value, *hops[0])]
    first, second = hops[-2:]
    diagonal = (first[0] | second[0], first[1] | second[1])
    return [value, swap_by(value, *first), swap_by(value, *second), swap_by(value, *diagonal)]


def tile_list(code, alive, parts, after):
    slots = code.shape[0]
    code = jnp.where(alive, code, (1 << 30) + jnp.arange(slots, dtype=jnp.int32))
    rank = jnp.sum((code[None, :] < code[:, None]).astype(jnp.int32), axis=1)
    places = jnp.arange(slots, dtype=jnp.int32)
    hit = (rank[None, :] == places[:, None]) & alive[None, :]
    ordered = jnp.sum(jnp.where(hit, code[None, :] - after, 0), axis=1) + after
    return place * (ordered // parts) + ordered % parts


def shards(rows, cols, emb_source, emb_target, source_mass, target_mass, start_potential, support, count):
    row = lax.axis_index("row").astype(jnp.int32)
    side, level = row % 2, row // 2
    core = lax.axis_index("col").astype(jnp.int32) % 2
    here = jnp.stack([side, level, core])
    levels = rows // 2
    per = emb_target.shape[0] // BLOCK
    own_sources = emb_source.shape[0] // BLOCK
    sources, targets = 2 * own_sources, levels * per

    order = list(range(0, levels, 2)) + list(range(levels - 1 - levels % 2, 0, -2))
    after = {order[k]: order[(k + 1) % levels] for k in range(levels)}
    onward = [(2 * z + s, 2 * after[z] + s) for z in range(levels) for s in range(2)]
    back = [(b, a) for a, b in onward]
    tgts, steps = [emb_target.T], [0]
    ahead = behind = tgts[0]
    for step in range(1, levels // 2 + 1):
        ahead = lax.ppermute(ahead, "row", onward)
        tgts.append(ahead)
        steps.append(-step)
        if 2 * step < levels:
            behind = lax.ppermute(behind, "row", back)
            tgts.append(behind)
            steps.append(step)

    swap_by = lambda value, row_bit, col_bit: swap(value, rows, cols, row_bit, col_bit)
    depth = support.shape[2]
    slots = sources * depth
    named = support.reshape(own_sources, depth)
    named = jnp.where(jnp.arange(depth, dtype=jnp.int32)[None, :] < count, named, -1)
    mine = jnp.concatenate([source_mass.reshape(own_sources, BLOCK), named.astype(jnp.float32)], axis=1)

    xt, mine = lax.optimization_barrier((emb_source.T, mine))
    theirs = swap_by(mine, 1, 0)
    half = xt.shape[1] // 2
    part = lax.dynamic_slice(xt, (jnp.int32(0), core * half), (xt.shape[0], half))
    part = swap_by(part, 1, 0)
    srcs = [xt, part, swap_by(part, 0, 1)]

    theirs, tgts[1] = lax.optimization_barrier((theirs, tgts[1]))
    pair = jnp.concatenate([jnp.where(side == 0, mine, theirs), jnp.where(side == 0, theirs, mine)])
    s_mass = pair[:, :BLOCK]
    named = pair[:, BLOCK:].astype(jnp.int32).reshape(slots)

    def of_side(whole):
        return lax.dynamic_index_in_dim(whole.reshape(levels, 2, per, BLOCK), side, 1, False).reshape(targets, BLOCK)

    alive = (named >= 0) & ((named // per) % 2 == side)
    t_ids = (named // (2 * per)) * per + named % per
    s_ids = jnp.arange(slots, dtype=jnp.int32) // depth
    live = jnp.sum(alive.astype(jnp.int32)).reshape(1)
    last = jnp.full((pad,), place, jnp.int32)
    by_source = tile_list(s_ids * targets + t_ids, alive, targets, sources * targets)
    by_source = jnp.concatenate([live, by_source, last * sources])
    by_target = tile_list(t_ids * sources + s_ids, alive, sources, sources * targets)
    by_target = jnp.concatenate([live, by_target, last * targets])
    by_source, by_target = lax.optimization_barrier((by_source, by_target))
    t_mass = of_side(target_mass)

    col_bits = [1 << k for k in range((cols - 1).bit_length())]
    row_bits = [1 << k for k in range((rows - 1).bit_length())]
    s_hops = [(0, bit) for bit in col_bits] + [(1, 0)]
    t_hops = [(bit, 0) for bit in row_bits[1:]]

    lse, ysq, xb, yb = first_pass(
        by_source, here, of_side(start_potential), srcs, tgts, steps, sources, targets, "source_first"
    )
    (lse,) = later_pass(by_target, exchange(lse, s_hops, swap_by), s_mass, xb, yb, False, "target_first")
    (lse,) = later_pass(by_source, exchange(lse, t_hops, swap_by), t_mass, yb, xb, False, "source_second")
    lse, pot = later_pass(by_target, exchange(lse, s_hops, swap_by), s_mass, xb, yb, True, "target_second")

    lse = lse - (eps * jnp.log(t_mass) + 0.5 * ysq)
    for hop in t_hops[:-1]:
        lse = merge(lse, swap_by(lse, *hop))
    last = t_hops[-1][0]
    own = merge(lse, swap_by(lse, last, 0)).reshape(levels, 1, per, BLOCK)
    other = merge(swap_by(lse, 1, 0), swap_by(lse, last | 1, 0)).reshape(levels, 1, per, BLOCK)
    second_g = -jnp.concatenate([jnp.where(side == 0, own, other), jnp.where(side == 0, other, own)], axis=1)
    xsq = squares(xt).reshape(own_sources, BLOCK)
    second_f = lax.dynamic_slice(pot, (side * own_sources, jnp.int32(0)), (own_sources, BLOCK)) + 0.5 * xsq
    return second_f.reshape(-1), second_g.reshape(-1)


def solution(mesh):
    in_specs = (
        P("row", None),
        P(("col", "row"), None),
        P("row"),
        P("col"),
        P("col"),
        P("row", "col", None),
        P("row", "col"),
    )
    out_specs = (P("row"), P("col"))
    body = functools.partial(shards, mesh.shape["row"], mesh.shape["col"])
    return jax.shard_map(body, mesh=mesh, in_specs=in_specs, out_specs=out_specs, check_vma=False)
```

```python
import functools

import jax
import jax.numpy as jnp
from jax import lax
from jax.experimental import pallas as pl
from jax.experimental.pallas import tpu as pltpu
from jax.sharding import PartitionSpec as P

BLOCK = 128
eps = 0.05
scale = 1.4426950408889634 / eps
unit = eps * 0.6931471805599453
floor = -1e30
turn = 16
longest = 64
pad = turn
place_bits = 12
place = 1 << place_bits


def merge(first, second, third=None, fourth=None):
    peak = jnp.maximum(first, second)
    if third is not None:
        peak = jnp.maximum(peak, jnp.maximum(third, fourth))
    total = jnp.exp2((first - peak) * scale) + jnp.exp2((second - peak) * scale)
    if third is not None:
        total += jnp.exp2((third - peak) * scale) + jnp.exp2((fourth - peak) * scale)
    return peak + unit * jnp.log2(total)


def squares(block):
    wide = block.astype(jnp.float32)
    return jnp.sum(wide * wide, axis=0, keepdims=True)


def rows_of(first, count, stride):
    return pl.ds(pl.multiple_of(first, 8), count) if stride == 1 else pl.ds(first, count, stride)


def store_split(tails, i, pot):
    first = pot.astype(jnp.bfloat16).astype(jnp.float32)
    rest = pot - first
    second = rest.astype(jnp.bfloat16).astype(jnp.float32)
    for k, part in enumerate((first, second, rest - second)):
        tails[pl.ds(i * 64 + k, 8, stride=8), :] = part


def one_rows():
    rows = lax.broadcasted_iota(jnp.int32, (16, BLOCK), 0)
    return jnp.where(rows < 3, 1.0, 0.0).astype(jnp.bfloat16)


def fetch(tiles_in, listed, arrived):
    return pltpu.make_async_copy(tiles_in, listed, arrived)


def tiles_lse(tiles_in, listed, arrived, lhs, tails, rhs, top, tot, out):
    ones = one_rows()
    zeros = jnp.zeros((8, BLOCK), jnp.float32)
    end = rhs.shape[0] - 1
    top[...] = jnp.full(top.shape, floor, jnp.float32)
    tot[...] = jnp.full(tot.shape, 0.125, jnp.float32)
    fetch(tiles_in, listed, arrived).wait()
    turns = (listed[0] + turn - 1) // turn

    def tiles(first, count, carry):
        last, run, total = carry
        for k in range(count):
            code = listed[1 + first + k]
            a, b = code & (place - 1), code >> place_bits
            tail = jnp.concatenate([tails[rows_of(a * 8, 8, 1), :], zeros]).astype(jnp.bfloat16)
            left = jnp.concatenate([lhs[a], tail], axis=0)
            right = jnp.concatenate([rhs[jnp.minimum(b, end)], ones], axis=0)
            z = lax.dot_general(left, right, (((0,), (0,)), ((), ())), preferred_element_type=jnp.float32)
            z = z.reshape(BLOCK // 8, 8, BLOCK)
            peak = jnp.max(z, axis=0)
            same = b == last
            joint = jnp.where(same, jnp.maximum(run, peak), peak)
            part = jnp.sum(jnp.exp2((z - joint) * scale), axis=0)
            total = jnp.where(same, total * jnp.exp2((run - joint) * scale), 0.0) + part
            top[rows_of(b * 8, 8, 1), :] = joint
            tot[rows_of(b * 8, 8, 1), :] = total
            last, run = b, joint
        return last, run, total

    def loop(first, count, size, carry):
        return lax.fori_loop(0, count, lambda i, held: tiles(first + i * size, size, held), carry)

    many = turns // (longest // turn)
    left_over = turns - many * (longest // turn)
    carry = loop(0, many, longest, (jnp.int32(-1), zeros, zeros))
    done = many * longest
    carry = loop(done, left_over // 2, 2 * turn, carry)
    done += (left_over // 2) * 2 * turn
    loop(done, lax.rem(left_over, 2), turn, carry)

    for i in range(out.shape[0] // 8):
        peaks = [top[pl.ds(i * 64 + k, 8, stride=8), :] for k in range(8)]
        peak = functools.reduce(jnp.maximum, peaks)
        total = 0.0
        for k in range(8):
            total += tot[pl.ds(i * 64 + k, 8, stride=8), :] * jnp.exp2((peaks[k] - peak) * scale)
        out[i * 8 : i * 8 + 8, :] = peak + unit * jnp.log2(total)


def ring_place(level, levels):
    return jnp.where(level % 2 == 0, level // 2, levels - (level + 1) // 2)


def ring_level(place, levels):
    place = lax.rem(place + levels, levels)
    return jnp.where(place < (levels + 1) // 2, 2 * place, 2 * (levels - place) - 1)


def first_kernel(n_src, n_tgt, levels, steps, here, tiles_in, pot_in, *refs):
    srcs, refs = refs[:n_src], refs[n_src:]
    tgts, refs = refs[:n_tgt], refs[n_tgt:]
    out, ysq, xb, yb, listed, arrived, tails, top, tot = refs
    fetch(tiles_in, listed, arrived).start()
    side, level, core = here[0], here[1], here[2]
    half = srcs[1].shape[1]
    far = 2 - 2 * side
    pieces = ((srcs[0], 0, 2 * side), (srcs[0], half, 2 * side + 1), (srcs[1], 0, far + core), (srcs[2], 0, far + 1 - core))
    for part, first, where in pieces:
        for j in range(half // BLOCK):
            xb[where * (half // BLOCK) + j] = part[:, first + j * BLOCK : first + (j + 1) * BLOCK]
    per = tgts[0].shape[1] // BLOCK
    for part, step in zip(tgts, steps):
        where = ring_level(ring_place(level, levels) + step, levels)
        for j in range(per):
            block = part[:, j * BLOCK : (j + 1) * BLOCK]
            yb[where * per + j] = block
            ysq[pl.ds(where * per + j, 1), :] = squares(block)
    tails[...] = jnp.zeros(tails.shape, jnp.float32)
    for i in range(yb.shape[0] // 8):
        rows = slice(i * 8, i * 8 + 8)
        store_split(tails, i, pot_in[rows, :] - 0.5 * ysq[rows, :])
    tiles_lse(tiles_in, listed, arrived, yb, tails, xb, top, tot, out)


def later_kernel(n_parts, keep, tiles_in, *refs):
    parts, refs = refs[:n_parts], refs[n_parts:]
    (mass, lhs, rhs, out), refs = refs[:4], refs[4:]
    if keep:
        (pot_out,), refs = refs[:1], refs[1:]
    listed, arrived, tails, top, tot = refs
    fetch(tiles_in, listed, arrived).start()
    tails[...] = jnp.zeros(tails.shape, jnp.float32)
    for i in range(lhs.shape[0] // 8):
        rows = slice(i * 8, i * 8 + 8)
        pot = unit * jnp.log2(mass[rows, :]) - merge(*[part[rows, :] for part in parts])
        if keep:
            pot_out[rows, :] = pot
        store_split(tails, i, pot)
    tiles_lse(tiles_in, listed, arrived, lhs, tails, rhs, top, tot, out)


vmem = pl.BlockSpec(memory_space=pltpu.VMEM)
smem = pl.BlockSpec(memory_space=pltpu.SMEM)


def tile_scratch(blocks_a, blocks_b, listed):
    return [
        pltpu.SMEM((listed,), jnp.int32),
        pltpu.SemaphoreType.DMA,
        pltpu.VMEM((blocks_a * 8, BLOCK), jnp.float32),
        pltpu.VMEM((blocks_b * 8 + 8, BLOCK), jnp.float32),
        pltpu.VMEM((blocks_b * 8 + 8, BLOCK), jnp.float32),
    ]


def first_pass(listed, here, pot, srcs, tgts, steps, sources, targets, name):
    n_src, n_tgt = len(srcs), len(tgts)
    shape = jax.ShapeDtypeStruct
    return pl.pallas_call(
        functools.partial(first_kernel, n_src, n_tgt, targets * BLOCK // tgts[0].shape[1], steps),
        out_shape=[
            shape((sources, BLOCK), jnp.float32),
            shape((targets, BLOCK), jnp.float32),
            shape((sources, 64, BLOCK), jnp.bfloat16),
            shape((targets, 64, BLOCK), jnp.bfloat16),
        ],
        in_specs=[smem, vmem, vmem] + [vmem] * (n_src + n_tgt),
        out_specs=[vmem] * 4,
        scratch_shapes=tile_scratch(targets, sources, listed.shape[0]),
        compiler_params=pltpu.CompilerParams(vmem_limit_bytes=32 * 1024 * 1024),
        name=name,
    )(here, listed, pot, *srcs, *tgts)


def later_pass(listed, parts, mass, lhs, rhs, keep, name):
    blocks_a, blocks_b = lhs.shape[0], rhs.shape[0]
    shapes = [(blocks_b, BLOCK)] + [(blocks_a, BLOCK)] * keep
    return pl.pallas_call(
        functools.partial(later_kernel, len(parts), keep),
        out_shape=[jax.ShapeDtypeStruct(shape, jnp.float32) for shape in shapes],
        in_specs=[vmem] + [vmem] * (len(parts) + 3),
        out_specs=[vmem] * len(shapes),
        scratch_shapes=tile_scratch(blocks_a, blocks_b, listed.shape[0]),
        compiler_params=pltpu.CompilerParams(vmem_limit_bytes=32 * 1024 * 1024),
        name=name,
    )(listed, *parts, mass, lhs, rhs)


def swap(value, rows, cols, row_bit, col_bit):
    if not col_bit:
        return lax.ppermute(value, "row", [(i, i ^ row_bit) for i in range(rows)])
    if not row_bit:
        return lax.ppermute(value, "col", [(i, i ^ col_bit) for i in range(cols)])
    pairs = [(i * cols + j, (i ^ row_bit) * cols + (j ^ col_bit)) for i in range(rows) for j in range(cols)]
    return lax.ppermute(value, ("row", "col"), pairs)


def exchange(value, hops, swap_by):
    for hop in hops[:-2]:
        value = merge(value, swap_by(value, *hop))
    if len(hops) == 1:
        return [value, swap_by(value, *hops[0])]
    first, second = hops[-2:]
    diagonal = (first[0] | second[0], first[1] | second[1])
    return [value, swap_by(value, *first), swap_by(value, *second), swap_by(value, *diagonal)]


def ranked(code, alive):
    code = jnp.where(alive, code, (1 << 30) + jnp.arange(code.shape[0], dtype=jnp.int32))
    return code, jnp.sum((code[None, :] < code[:, None]).astype(jnp.int32), axis=1)


def tile_list(code, rank, alive, parts, after):
    places = jnp.arange(code.shape[0], dtype=jnp.int32)
    hit = (rank[None, :] == places[:, None]) & alive[None, :]
    ordered = jnp.sum(jnp.where(hit, code[None, :] - after, 0), axis=1) + after
    return place * (ordered // parts) + ordered % parts


def shards(rows, cols, emb_source, emb_target, source_mass, target_mass, start_potential, support, count):
    row = lax.axis_index("row").astype(jnp.int32)
    side, level = row % 2, row // 2
    core = lax.axis_index("col").astype(jnp.int32) % 2
    here = jnp.stack([side, level, core])
    levels = rows // 2
    per = emb_target.shape[0] // BLOCK
    own_sources = emb_source.shape[0] // BLOCK
    sources, targets = 2 * own_sources, levels * per

    order = list(range(0, levels, 2)) + list(range(levels - 1 - levels % 2, 0, -2))
    after = {order[k]: order[(k + 1) % levels] for k in range(levels)}
    onward = [(2 * z + s, 2 * after[z] + s) for z in range(levels) for s in range(2)]
    back = [(b, a) for a, b in onward]
    tgts, steps = [emb_target.T], [0]
    ahead = behind = tgts[0]
    for step in range(1, levels // 2 + 1):
        ahead = lax.ppermute(ahead, "row", onward)
        tgts.append(ahead)
        steps.append(-step)
        if 2 * step < levels:
            behind = lax.ppermute(behind, "row", back)
            tgts.append(behind)
            steps.append(step)

    swap_by = lambda value, row_bit, col_bit: swap(value, rows, cols, row_bit, col_bit)
    depth = support.shape[2]
    slots = sources * depth
    named = support.reshape(own_sources, depth)
    named = jnp.where(jnp.arange(depth, dtype=jnp.int32)[None, :] < count, named, -1)
    mine = jnp.concatenate([source_mass.reshape(own_sources, BLOCK), named.astype(jnp.float32)], axis=1)

    xt, mine = lax.optimization_barrier((emb_source.T, mine))
    theirs = swap_by(mine, 1, 0)
    half = xt.shape[1] // 2
    part = lax.dynamic_slice(xt, (jnp.int32(0), core * half), (xt.shape[0], half))
    part = swap_by(part, 1, 0)
    srcs = [xt, part, swap_by(part, 0, 1)]

    pair = jnp.concatenate([jnp.where(side == 0, mine, theirs), jnp.where(side == 0, theirs, mine)])
    s_mass = pair[:, :BLOCK]
    named = pair[:, BLOCK:].astype(jnp.int32).reshape(slots)

    def of_side(whole):
        return lax.dynamic_index_in_dim(whole.reshape(levels, 2, per, BLOCK), side, 1, False).reshape(targets, BLOCK)

    alive = (named >= 0) & ((named // per) % 2 == side)
    t_ids = (named // (2 * per)) * per + named % per
    s_ids = jnp.arange(slots, dtype=jnp.int32) // depth
    live = jnp.sum(alive.astype(jnp.int32)).reshape(1)
    last = jnp.full((pad,), place, jnp.int32)
    s_code, s_rank = ranked(s_ids * targets + t_ids, alive)
    t_code, t_rank = ranked(t_ids * sources + s_ids, alive)
    s_rank, t_rank, tgts[1] = lax.optimization_barrier((s_rank, t_rank, tgts[1]))
    by_source = tile_list(s_code, s_rank, alive, targets, sources * targets)
    by_source = jnp.concatenate([live, by_source, last * sources])
    by_target = tile_list(t_code, t_rank, alive, sources, sources * targets)
    by_target = jnp.concatenate([live, by_target, last * targets])
    by_source, by_target = lax.optimization_barrier((by_source, by_target))
    t_mass = of_side(target_mass)

    col_bits = [1 << k for k in range((cols - 1).bit_length())]
    row_bits = [1 << k for k in range((rows - 1).bit_length())]
    s_hops = [(0, bit) for bit in col_bits] + [(1, 0)]
    t_hops = [(bit, 0) for bit in row_bits[1:]]

    lse, ysq, xb, yb = first_pass(
        by_source, here, of_side(start_potential), srcs, tgts, steps, sources, targets, "source_first"
    )
    (lse,) = later_pass(by_target, exchange(lse, s_hops, swap_by), s_mass, xb, yb, False, "target_first")
    (lse,) = later_pass(by_source, exchange(lse, t_hops, swap_by), t_mass, yb, xb, False, "source_second")
    lse, pot = later_pass(by_target, exchange(lse, s_hops, swap_by), s_mass, xb, yb, True, "target_second")

    lse = lse - (eps * jnp.log(t_mass) + 0.5 * ysq)
    for hop in t_hops[:-1]:
        lse = merge(lse, swap_by(lse, *hop))
    last = t_hops[-1][0]
    own = merge(lse, swap_by(lse, last, 0)).reshape(levels, 1, per, BLOCK)
    other = merge(swap_by(lse, 1, 0), swap_by(lse, last | 1, 0)).reshape(levels, 1, per, BLOCK)
    second_g = -jnp.concatenate([jnp.where(side == 0, own, other), jnp.where(side == 0, other, own)], axis=1)
    xsq = squares(xt).reshape(own_sources, BLOCK)
    second_f = lax.dynamic_slice(pot, (side * own_sources, jnp.int32(0)), (own_sources, BLOCK)) + 0.5 * xsq
    return second_f.reshape(-1), second_g.reshape(-1)


def solution(mesh):
    in_specs = (
        P("row", None),
        P(("col", "row"), None),
        P("row"),
        P("col"),
        P("col"),
        P("row", "col", None),
        P("row", "col"),
    )
    out_specs = (P("row"), P("col"))
    body = functools.partial(shards, mesh.shape["row"], mesh.shape["col"])
    return jax.shard_map(body, mesh=mesh, in_specs=in_specs, out_specs=out_specs, check_vma=False)
```

```python
import functools

import jax
import jax.numpy as jnp
from jax import lax
from jax.experimental import pallas as pl
from jax.experimental.pallas import tpu as pltpu
from jax.sharding import PartitionSpec as P

BLOCK = 128
eps = 0.05
scale = 1.4426950408889634 / eps
unit = eps * 0.6931471805599453
floor = -1e30
turn = 16
longest = 64
pad = turn
place_bits = 12
place = 1 << place_bits


def merge(first, second, third=None, fourth=None):
    peak = jnp.maximum(first, second)
    if third is not None:
        peak = jnp.maximum(peak, jnp.maximum(third, fourth))
    total = jnp.exp2((first - peak) * scale) + jnp.exp2((second - peak) * scale)
    if third is not None:
        total += jnp.exp2((third - peak) * scale) + jnp.exp2((fourth - peak) * scale)
    return peak + unit * jnp.log2(total)


def squares(block):
    wide = block.astype(jnp.float32)
    return jnp.sum(wide * wide, axis=0, keepdims=True)


def rows_of(first, count, stride):
    return pl.ds(pl.multiple_of(first, 8), count) if stride == 1 else pl.ds(first, count, stride)


def store_split(tails, i, pot):
    first = pot.astype(jnp.bfloat16).astype(jnp.float32)
    rest = pot - first
    second = rest.astype(jnp.bfloat16).astype(jnp.float32)
    for k, part in enumerate((first, second, rest - second)):
        tails[pl.ds(i * 64 + k, 8, stride=8), :] = part


def one_rows():
    rows = lax.broadcasted_iota(jnp.int32, (16, BLOCK), 0)
    return jnp.where(rows < 3, 1.0, 0.0).astype(jnp.bfloat16)


def fetch(tiles_in, listed, arrived):
    return pltpu.make_async_copy(tiles_in, listed, arrived)


def tiles_lse(tiles_in, listed, arrived, lhs, tails, rhs, top, tot, out):
    ones = one_rows()
    zeros = jnp.zeros((8, BLOCK), jnp.float32)
    end = rhs.shape[0] - 1
    top[...] = jnp.full(top.shape, floor, jnp.float32)
    tot[...] = jnp.full(tot.shape, 0.125, jnp.float32)
    fetch(tiles_in, listed, arrived).wait()
    turns = (listed[0] + turn - 1) // turn

    def tiles(first, count, carry):
        last, run, total = carry
        for k in range(count):
            code = listed[1 + first + k]
            a, b = code & (place - 1), code >> place_bits
            tail = jnp.concatenate([tails[rows_of(a * 8, 8, 1), :], zeros]).astype(jnp.bfloat16)
            left = jnp.concatenate([lhs[a], tail], axis=0)
            right = jnp.concatenate([rhs[jnp.minimum(b, end)], ones], axis=0)
            z = lax.dot_general(left, right, (((0,), (0,)), ((), ())), preferred_element_type=jnp.float32)
            z = z.reshape(BLOCK // 8, 8, BLOCK)
            peak = jnp.max(z, axis=0)
            same = b == last
            joint = jnp.where(same, jnp.maximum(run, peak), peak)
            part = jnp.sum(jnp.exp2((z - joint) * scale), axis=0)
            total = jnp.where(same, total * jnp.exp2((run - joint) * scale), 0.0) + part
            top[rows_of(b * 8, 8, 1), :] = joint
            tot[rows_of(b * 8, 8, 1), :] = total
            last, run = b, joint
        return last, run, total

    def loop(first, count, size, carry):
        return lax.fori_loop(0, count, lambda i, held: tiles(first + i * size, size, held), carry)

    many = turns // (longest // turn)
    left_over = turns - many * (longest // turn)
    carry = loop(0, many, longest, (jnp.int32(-1), zeros, zeros))
    done = many * longest
    carry = loop(done, left_over // 2, 2 * turn, carry)
    done += (left_over // 2) * 2 * turn
    loop(done, lax.rem(left_over, 2), turn, carry)

    for i in range(out.shape[0] // 8):
        peaks = [top[pl.ds(i * 64 + k, 8, stride=8), :] for k in range(8)]
        peak = functools.reduce(jnp.maximum, peaks)
        total = 0.0
        for k in range(8):
            total += tot[pl.ds(i * 64 + k, 8, stride=8), :] * jnp.exp2((peaks[k] - peak) * scale)
        out[i * 8 : i * 8 + 8, :] = peak + unit * jnp.log2(total)


def ring_place(level, levels):
    return jnp.where(level % 2 == 0, level // 2, levels - (level + 1) // 2)


def ring_level(place, levels):
    place = lax.rem(place + levels, levels)
    return jnp.where(place < (levels + 1) // 2, 2 * place, 2 * (levels - place) - 1)


def first_kernel(n_src, n_tgt, levels, steps, here, tiles_in, pot_in, *refs):
    srcs, refs = refs[:n_src], refs[n_src:]
    tgts, refs = refs[:n_tgt], refs[n_tgt:]
    out, ysq, xb, yb, listed, arrived, tails, top, tot = refs
    fetch(tiles_in, listed, arrived).start()
    side, level, core = here[0], here[1], here[2]
    half = srcs[1].shape[1]
    far = 2 - 2 * side
    pieces = ((srcs[0], 0, 2 * side), (srcs[0], half, 2 * side + 1), (srcs[1], 0, far + core), (srcs[2], 0, far + 1 - core))
    for part, first, where in pieces:
        for j in range(half // BLOCK):
            xb[where * (half // BLOCK) + j] = part[:, first + j * BLOCK : first + (j + 1) * BLOCK]
    per = tgts[0].shape[1] // BLOCK
    for part, step in zip(tgts, steps):
        where = ring_level(ring_place(level, levels) + step, levels)
        for j in range(per):
            block = part[:, j * BLOCK : (j + 1) * BLOCK]
            yb[where * per + j] = block
            ysq[pl.ds(where * per + j, 1), :] = squares(block)
    tails[...] = jnp.zeros(tails.shape, jnp.float32)
    for i in range(yb.shape[0] // 8):
        rows = slice(i * 8, i * 8 + 8)
        store_split(tails, i, pot_in[rows, :] - 0.5 * ysq[rows, :])
    tiles_lse(tiles_in, listed, arrived, yb, tails, xb, top, tot, out)


def later_kernel(n_parts, keep, tiles_in, *refs):
    parts, refs = refs[:n_parts], refs[n_parts:]
    (mass, lhs, rhs, out), refs = refs[:4], refs[4:]
    if keep:
        (pot_out,), refs = refs[:1], refs[1:]
    listed, arrived, tails, top, tot = refs
    fetch(tiles_in, listed, arrived).start()
    tails[...] = jnp.zeros(tails.shape, jnp.float32)
    for i in range(lhs.shape[0] // 8):
        rows = slice(i * 8, i * 8 + 8)
        pot = unit * jnp.log2(mass[rows, :]) - merge(*[part[rows, :] for part in parts])
        if keep:
            pot_out[rows, :] = pot
        store_split(tails, i, pot)
    tiles_lse(tiles_in, listed, arrived, lhs, tails, rhs, top, tot, out)


vmem = pl.BlockSpec(memory_space=pltpu.VMEM)
smem = pl.BlockSpec(memory_space=pltpu.SMEM)


def tile_scratch(blocks_a, blocks_b, listed):
    return [
        pltpu.SMEM((listed,), jnp.int32),
        pltpu.SemaphoreType.DMA,
        pltpu.VMEM((blocks_a * 8, BLOCK), jnp.float32),
        pltpu.VMEM((blocks_b * 8 + 8, BLOCK), jnp.float32),
        pltpu.VMEM((blocks_b * 8 + 8, BLOCK), jnp.float32),
    ]


def first_pass(listed, here, pot, srcs, tgts, steps, sources, targets, name):
    n_src, n_tgt = len(srcs), len(tgts)
    shape = jax.ShapeDtypeStruct
    return pl.pallas_call(
        functools.partial(first_kernel, n_src, n_tgt, targets * BLOCK // tgts[0].shape[1], steps),
        out_shape=[
            shape((sources, BLOCK), jnp.float32),
            shape((targets, BLOCK), jnp.float32),
            shape((sources, 64, BLOCK), jnp.bfloat16),
            shape((targets, 64, BLOCK), jnp.bfloat16),
        ],
        in_specs=[smem, vmem, vmem] + [vmem] * (n_src + n_tgt),
        out_specs=[vmem] * 4,
        scratch_shapes=tile_scratch(targets, sources, listed.shape[0]),
        compiler_params=pltpu.CompilerParams(vmem_limit_bytes=32 * 1024 * 1024),
        name=name,
    )(here, listed, pot, *srcs, *tgts)


def later_pass(listed, parts, mass, lhs, rhs, keep, name):
    blocks_a, blocks_b = lhs.shape[0], rhs.shape[0]
    shapes = [(blocks_b, BLOCK)] + [(blocks_a, BLOCK)] * keep
    return pl.pallas_call(
        functools.partial(later_kernel, len(parts), keep),
        out_shape=[jax.ShapeDtypeStruct(shape, jnp.float32) for shape in shapes],
        in_specs=[vmem] + [vmem] * (len(parts) + 3),
        out_specs=[vmem] * len(shapes),
        scratch_shapes=tile_scratch(blocks_a, blocks_b, listed.shape[0]),
        compiler_params=pltpu.CompilerParams(vmem_limit_bytes=32 * 1024 * 1024),
        name=name,
    )(listed, *parts, mass, lhs, rhs)


def swap(value, rows, cols, row_bit, col_bit):
    if not col_bit:
        return lax.ppermute(value, "row", [(i, i ^ row_bit) for i in range(rows)])
    if not row_bit:
        return lax.ppermute(value, "col", [(i, i ^ col_bit) for i in range(cols)])
    pairs = [(i * cols + j, (i ^ row_bit) * cols + (j ^ col_bit)) for i in range(rows) for j in range(cols)]
    return lax.ppermute(value, ("row", "col"), pairs)


def exchange(value, hops, swap_by):
    for hop in hops[:-2]:
        value = merge(value, swap_by(value, *hop))
    if len(hops) == 1:
        return [value, swap_by(value, *hops[0])]
    first, second = hops[-2:]
    diagonal = (first[0] | second[0], first[1] | second[1])
    return [value, swap_by(value, *first), swap_by(value, *second), swap_by(value, *diagonal)]


def tile_list(code, alive, parts, after):
    slots = code.shape[0]
    code = jnp.where(alive, code, (1 << 30) + jnp.arange(slots, dtype=jnp.int32))
    rank = jnp.sum((code[None, :] < code[:, None]).astype(jnp.int32), axis=1)
    places = jnp.arange(slots, dtype=jnp.int32)
    hit = (rank[None, :] == places[:, None]) & alive[None, :]
    ordered = jnp.sum(jnp.where(hit, code[None, :] - after, 0), axis=1) + after
    return place * (ordered // parts) + ordered % parts


def shards(rows, cols, emb_source, emb_target, source_mass, target_mass, start_potential, support, count):
    row = lax.axis_index("row").astype(jnp.int32)
    side, level = row % 2, row // 2
    core = lax.axis_index("col").astype(jnp.int32) % 2
    here = jnp.stack([side, level, core])
    levels = rows // 2
    per = emb_target.shape[0] // BLOCK
    own_sources = emb_source.shape[0] // BLOCK
    sources, targets = 2 * own_sources, levels * per

    order = list(range(0, levels, 2)) + list(range(levels - 1 - levels % 2, 0, -2))
    after = {order[k]: order[(k + 1) % levels] for k in range(levels)}
    onward = [(2 * z + s, 2 * after[z] + s) for z in range(levels) for s in range(2)]
    back = [(b, a) for a, b in onward]
    tgts, steps = [emb_target.T], [0]
    ahead = behind = tgts[0]
    for step in range(1, levels // 2 + 1):
        ahead = lax.ppermute(ahead, "row", onward)
        tgts.append(ahead)
        steps.append(-step)
        if 2 * step < levels:
            behind = lax.ppermute(behind, "row", back)
            tgts.append(behind)
            steps.append(step)

    swap_by = lambda value, row_bit, col_bit: swap(value, rows, cols, row_bit, col_bit)
    depth = support.shape[2]
    slots = sources * depth
    named = support.reshape(own_sources, depth)
    named = jnp.where(jnp.arange(depth, dtype=jnp.int32)[None, :] < count, named, -1)
    mine = jnp.concatenate([source_mass.reshape(own_sources, BLOCK), named.astype(jnp.float32)], axis=1)

    xt, mine = lax.optimization_barrier((emb_source.T, mine))
    theirs = swap_by(mine, 1, 0)
    half = xt.shape[1] // 2
    part = lax.dynamic_slice(xt, (jnp.int32(0), core * half), (xt.shape[0], half))
    part = swap_by(part, 1, 0)
    srcs = [xt, part, swap_by(part, 0, 1)]

    theirs, tgts[1] = lax.optimization_barrier((theirs, tgts[1]))
    pair = jnp.concatenate([jnp.where(side == 0, mine, theirs), jnp.where(side == 0, theirs, mine)])
    s_mass = pair[:, :BLOCK]
    named = pair[:, BLOCK:].astype(jnp.int32).reshape(slots)

    def of_side(whole):
        return lax.dynamic_index_in_dim(whole.reshape(levels, 2, per, BLOCK), side, 1, False).reshape(targets, BLOCK)

    alive = (named >= 0) & ((named // per) % 2 == side)
    t_ids = (named // (2 * per)) * per + named % per
    s_ids = jnp.arange(slots, dtype=jnp.int32) // depth
    live = jnp.sum(alive.astype(jnp.int32)).reshape(1)
    last = jnp.full((pad,), place, jnp.int32)
    by_source = tile_list(s_ids * targets + t_ids, alive, targets, sources * targets)
    by_source = jnp.concatenate([live, by_source, last * sources])
    by_target = tile_list(t_ids * sources + s_ids, alive, sources, sources * targets)
    by_target = jnp.concatenate([live, by_target, last * targets])
    by_source, by_target = lax.optimization_barrier((by_source, by_target))
    t_mass = of_side(target_mass)

    col_bits = [1 << k for k in range((cols - 1).bit_length())]
    row_bits = [1 << k for k in range((rows - 1).bit_length())]
    s_hops = [(0, bit) for bit in col_bits] + [(1, 0)]
    t_hops = [(bit, 0) for bit in row_bits[1:]]

    lse, ysq, xb, yb = first_pass(
        by_source, here, of_side(start_potential), srcs, tgts, steps, sources, targets, "source_first"
    )
    (lse,) = later_pass(by_target, exchange(lse, s_hops, swap_by), s_mass, xb, yb, False, "target_first")
    (lse,) = later_pass(by_source, exchange(lse, t_hops, swap_by), t_mass, yb, xb, False, "source_second")
    lse, pot = later_pass(by_target, exchange(lse, s_hops, swap_by), s_mass, xb, yb, True, "target_second")

    lse = lse - (eps * jnp.log(t_mass) + 0.5 * ysq)
    for hop in t_hops[1:]:
        lse = merge(lse, swap_by(lse, *hop))
    last = t_hops[0][0]
    own = merge(lse, swap_by(lse, last, 0)).reshape(levels, 1, per, BLOCK)
    other = merge(swap_by(lse, 1, 0), swap_by(lse, last | 1, 0)).reshape(levels, 1, per, BLOCK)
    second_g = -jnp.concatenate([jnp.where(side == 0, own, other), jnp.where(side == 0, other, own)], axis=1)
    xsq = squares(xt).reshape(own_sources, BLOCK)
    second_f = lax.dynamic_slice(pot, (side * own_sources, jnp.int32(0)), (own_sources, BLOCK)) + 0.5 * xsq
    return second_f.reshape(-1), second_g.reshape(-1)


def solution(mesh):
    in_specs = (
        P("row", None),
        P(("col", "row"), None),
        P("row"),
        P("col"),
        P("col"),
        P("row", "col", None),
        P("row", "col"),
    )
    out_specs = (P("row"), P("col"))
    body = functools.partial(shards, mesh.shape["row"], mesh.shape["col"])
    return jax.shard_map(body, mesh=mesh, in_specs=in_specs, out_specs=out_specs, check_vma=False)
```
